256 devices in a mesh: dp: 64 (over z, x, core), tensor: 4 (over y).
Axes of the slice: x: 4, y: 4, z: 8, core: 2. Of those that a mesh axis runs over, the one named last changes fastest.
Arguments:
- queries: bfloat16 [128, 256, 5120], P('dp', None, 'tensor'), may hold values from -5 to 5
- resp_keys: bfloat16 [128, 256, 1024], P('dp', None, 'tensor'), may hold values from -5 to 5
- response_values: bfloat16 [128, 256, 1024], P('dp', None, 'tensor'), may hold values from -5 to 5
- prompt_key_rows: bfloat16 [4096, 1024], P('dp', 'tensor'), may hold values from -5 to 5
- prompt_value_rows: bfloat16 [4096, 1024], P('dp', 'tensor'), may hold values from -5 to 5
- out_grad: bfloat16 [128, 256, 5120], P('dp', None, 'tensor'), may hold values from -5 to 5
- group_list: int32 [8, 16], replicated, may hold values from 0 to 127, as said below
- lengths: int32 [128], P('dp'), may hold values from 1 to 256, 24576 in all
Outputs:
- attn_out: bfloat16 [128, 256, 5120], P('dp', None, 'tensor')
- grad_queries: bfloat16 [128, 256, 5120], P('dp', None, 'tensor')
- grad_resp_keys: bfloat16 [128, 256, 1024], P('dp', None, 'tensor')
- grad_resp_values: bfloat16 [128, 256, 1024], P('dp', None, 'tensor')
- grad_prompt_keys: bfloat16 [4096, 1024], P('dp', 'tensor')
- grad_prompt_values: bfloat16 [4096, 1024], P('dp', 'tensor')
The draws below stay inside these ranges and needn't reach their ends.
Inputs may be any that keep to these rules, and one draw needn't show every extreme that they name: `group_list`: every response 0 to 127 appears exactly once. `lengths`: some response has 256 tokens.
All inputs are finite; a program needn't handle non-finite values. No bound on the sum of `lengths` on one device may be relied on, other than what follows from the above.
Results may differ from the reference program's by a relative error of at most 0.035.
Values may be sent and summed in bfloat16 or wider, within the bound.
No kernel may reach another device: no remote copies, remote signals or barrier semaphores. Data moves between devices by JAX's collectives and lax.ppermute only.
A program may use at most 128 MiB of HBM per device.

```python
import math
import jax
import jax.numpy as jnp
import numpy as np
from jax import lax

QUERY_HEADS = 40
KEY_VALUE_HEADS = 8
HEAD_SIZE = 128
GROUP = 16
RESPONSE_LENGTH = 256
RESPONSE_TOTAL = 128
PROMPT_TOTAL = 8
PROMPT_LENGTH = 512


def draw_queries(key, part):
    key = jax.random.fold_in(key, 11)
    sampled = jnp.clip(jax.random.normal(key, (RESPONSE_TOTAL, RESPONSE_LENGTH, QUERY_HEADS * HEAD_SIZE), jnp.float32), -5.0, 5.0)
    return sampled.astype(jnp.bfloat16)


def draw_resp_keys(key, part):
    key = jax.random.fold_in(key, 23)
    sampled = jnp.clip(jax.random.normal(key, (RESPONSE_TOTAL, RESPONSE_LENGTH, KEY_VALUE_HEADS * HEAD_SIZE), jnp.float32), -5.0, 5.0)
    return sampled.astype(jnp.bfloat16)


def draw_group_list(key, part):
    key = jax.random.fold_in(key, 37)
    order = jax.random.permutation(key, PROMPT_TOTAL * GROUP)
    return order.reshape(PROMPT_TOTAL, GROUP).astype(jnp.int32)


def block_levels(key, dims, pieces, low, high):
    loudness = 1.0
    for axis_at, blocks in pieces:
        steps = jax.random.uniform(jax.random.fold_in(jax.random.fold_in(key, 6), axis_at), (blocks,), jnp.float32, low / len(pieces), high / len(pieces))
        loudness = loudness * jnp.repeat(jnp.exp(steps), dims[axis_at] // blocks).reshape((-1,) + (1,) * (len(dims) - 1 - axis_at))
    return loudness


def split_up(count, total, limit, skew):
    portions = [(1 << 20) // math.isqrt(standing ** skew) + 1 for standing in range(2, count + 1)]
    surplus, counts = total - limit - (count - 1), [1] * (count - 1)
    while surplus > 0:
        movable = [i for i in range(count - 1) if counts[i] < limit]
        mass, left = sum([portions[i] for i in movable]), surplus
        for i in movable:
            more = min(limit - counts[i], max(1, left * portions[i] // mass), surplus)
            counts[i] = counts[i] + more
            surplus = surplus - more
    return np.array([limit] + counts)


def uneven_parts(own_key, count, total, reach, lean):
    if count == 2:
        one = jax.random.randint(own_key, (), max(1, total - reach), min(reach, total - 1) + 1)
        return jnp.stack([one, total - one])
    sizes = jnp.asarray(split_up(count, total, reach, lean), jnp.int32)
    twos = (count - 1) // 2
    donor, sink = sizes[1:1 + 2 * twos:2], sizes[2:2 + 2 * twos:2]
    room = jnp.minimum(donor - 1, reach - sink)
    passed = jax.random.randint(jax.random.fold_in(own_key, 1), (twos,), 0, 1 << 20) % (room + 1)
    sizes = sizes.at[1:1 + 2 * twos:2].set(donor - passed).at[2:2 + 2 * twos:2].set(sink + passed)
    return sizes[jax.random.permutation(jax.random.fold_in(own_key, 2), count)]


def bell_draw(stream_key, dims, deviation, most, pieces=(), held_as=jnp.bfloat16):
    loudness = block_levels(stream_key, dims, pieces, -0.22, 0.18) if pieces else 1.0
    values = jax.random.normal(stream_key, dims, jnp.float32) * deviation * loudness
    return jnp.minimum(jnp.maximum(values, -most), most).astype(held_as)


def setup_inputs(seed: int = 0) -> dict:
    seeds = jax.random.split(jax.random.key(seed), 9)
    queries = draw_queries(jax.random.fold_in(seeds[8], 71), 0)
    resp_keys = draw_resp_keys(jax.random.fold_in(seeds[8], 71), 0)
    response_values = bell_draw(seeds[2], (RESPONSE_TOTAL, RESPONSE_LENGTH, KEY_VALUE_HEADS * HEAD_SIZE), 1.0, 5.0, ((0, 64), (2, 4)))
    prompt_key_rows = bell_draw(seeds[3], (PROMPT_TOTAL * PROMPT_LENGTH, KEY_VALUE_HEADS * HEAD_SIZE), 1.0, 5.0, ((0, 64), (1, 4)))
    prompt_value_rows = bell_draw(seeds[4], (PROMPT_TOTAL * PROMPT_LENGTH, KEY_VALUE_HEADS * HEAD_SIZE), 1.0, 5.0, ((0, 64), (1, 4)))
    out_grad = bell_draw(seeds[5], (RESPONSE_TOTAL, RESPONSE_LENGTH, QUERY_HEADS * HEAD_SIZE), 1.0, 5.0, ((0, 64), (2, 4)))
    group_list = draw_group_list(jax.random.fold_in(seeds[8], 71), 0)
    lengths = uneven_parts(seeds[7], RESPONSE_TOTAL, RESPONSE_TOTAL * RESPONSE_LENGTH * 3 // 4, RESPONSE_LENGTH, 1).astype(jnp.int32)
    return {"queries": queries, "resp_keys": resp_keys, "response_values": response_values, "prompt_key_rows": prompt_key_rows, "prompt_value_rows": prompt_value_rows, "out_grad": out_grad, "group_list": group_list, "lengths": lengths}


def round_half(value):
    return lax.optimization_barrier(value.astype(jnp.bfloat16)).astype(jnp.float32)


def respond(single_query, single_key, single_value, prompt_key_block, prompt_value_block, single_gradient, length):
    token_rows = single_query.shape[0]
    heads_per_group = QUERY_HEADS // KEY_VALUE_HEADS
    score_scale = HEAD_SIZE ** -0.5
    query_head_rows = single_query.astype(jnp.float32).reshape(token_rows, KEY_VALUE_HEADS, heads_per_group, HEAD_SIZE)
    joined_keys = jnp.concatenate([prompt_key_block, single_key], 0).astype(jnp.float32).reshape(PROMPT_LENGTH + token_rows, KEY_VALUE_HEADS, HEAD_SIZE)
    joined_values = jnp.concatenate([prompt_value_block, single_value], 0).astype(jnp.float32).reshape(PROMPT_LENGTH + token_rows, KEY_VALUE_HEADS, HEAD_SIZE)
    scores = jnp.einsum("igtd,jgd->gtij", query_head_rows, joined_keys) * score_scale
    query_pos = jnp.arange(token_rows, dtype=jnp.int32)
    key_pos = jnp.arange(PROMPT_LENGTH + token_rows, dtype=jnp.int32) - PROMPT_LENGTH
    allowed = key_pos[None, :] <= query_pos[:, None]
    scores = jnp.where(allowed, scores, -jnp.inf)
    highest = jnp.max(scores, axis=-1, keepdims=True)
    log_total = highest + jnp.log(jnp.sum(jnp.exp(scores - highest), axis=-1, keepdims=True))
    valid_rows = (query_pos < length).astype(jnp.float32)[:, None]
    weights = jnp.exp(scores - log_total) * valid_rows
    weights_half = round_half(weights)
    attention_result = jnp.einsum("gtij,jgd->igtd", weights_half, joined_values).reshape(token_rows, QUERY_HEADS * HEAD_SIZE).astype(jnp.bfloat16)
    gradient_heads = single_gradient.astype(jnp.float32).reshape(token_rows, KEY_VALUE_HEADS, heads_per_group, HEAD_SIZE)
    head_results = attention_result.astype(jnp.float32).reshape(token_rows, KEY_VALUE_HEADS, heads_per_group, HEAD_SIZE)
    row_delta = jnp.transpose(jnp.sum(gradient_heads * head_results, axis=-1), (1, 2, 0))
    grad_weights = jnp.einsum("igtd,jgd->gtij", gradient_heads, joined_values)
    dscore = weights * (grad_weights - row_delta[..., None])
    dscore_half = round_half(dscore)
    grad_query = (jnp.einsum("gtij,jgd->igtd", dscore_half, joined_keys) * score_scale).reshape(token_rows, QUERY_HEADS * HEAD_SIZE).astype(jnp.bfloat16)
    grad_key = jnp.einsum("gtij,igtd->jgd", dscore_half, query_head_rows) * score_scale
    grad_value = jnp.einsum("gtij,igtd->jgd", weights_half, gradient_heads)
    key_value_width = KEY_VALUE_HEADS * HEAD_SIZE
    return attention_result, grad_query, grad_key.reshape(PROMPT_LENGTH + token_rows, key_value_width), grad_value.reshape(PROMPT_LENGTH + token_rows, key_value_width)


def reference(queries, resp_keys, response_values, prompt_key_rows, prompt_value_rows, out_grad, group_list, lengths):
    member = (group_list[:, :, None] == jnp.arange(RESPONSE_TOTAL, dtype=jnp.int32)[None, None, :]).astype(jnp.int32)
    prompt_of = jnp.sum(jnp.arange(PROMPT_TOTAL, dtype=jnp.int32)[:, None] * jnp.sum(member, axis=1), axis=0).astype(jnp.int32)
    key_value_width = KEY_VALUE_HEADS * HEAD_SIZE

    def step(totals, slot_at):
        total_k, total_v = totals
        row_start = (prompt_of[slot_at] * PROMPT_LENGTH).astype(jnp.int32)
        prompt_key_block = lax.dynamic_slice_in_dim(prompt_key_rows, row_start, PROMPT_LENGTH, 0)
        prompt_value_block = lax.dynamic_slice_in_dim(prompt_value_rows, row_start, PROMPT_LENGTH, 0)
        attention_result, grad_query, grad_key, grad_value = respond(queries[slot_at], resp_keys[slot_at], response_values[slot_at], prompt_key_block, prompt_value_block, out_grad[slot_at], lengths[slot_at])
        total_k = lax.dynamic_update_slice_in_dim(total_k, lax.dynamic_slice_in_dim(total_k, row_start, PROMPT_LENGTH, 0) + grad_key[:PROMPT_LENGTH], row_start, 0)
        total_v = lax.dynamic_update_slice_in_dim(total_v, lax.dynamic_slice_in_dim(total_v, row_start, PROMPT_LENGTH, 0) + grad_value[:PROMPT_LENGTH], row_start, 0)
        return (total_k, total_v), (attention_result, grad_query, grad_key[PROMPT_LENGTH:].astype(jnp.bfloat16), grad_value[PROMPT_LENGTH:].astype(jnp.bfloat16))

    zero_rows = jnp.zeros((PROMPT_TOTAL * PROMPT_LENGTH, key_value_width), jnp.float32)
    totals, stacked = lax.scan(step, (zero_rows, zero_rows), jnp.arange(RESPONSE_TOTAL, dtype=jnp.int32))
    return (stacked[0], stacked[1], stacked[2], stacked[3], totals[0].astype(jnp.bfloat16), totals[1].astype(jnp.bfloat16))
```

```python
import functools
import math

import jax
import jax.numpy as jnp
from jax import lax
from jax.experimental import pallas as pl
from jax.experimental.pallas import tpu as pltpu
from jax.sharding import PartitionSpec as P

HEAD_SIZE = 128
SCALE = HEAD_SIZE**-0.5
SCALE_LOG2 = SCALE * math.log2(math.e)
HALF = 128
NT = (((1,), (1,)), ((), ()))
NN = (((1,), (0,)), ((), ()))
TN = (((0,), (0,)), ((), ()))
f32 = jnp.float32
bf16 = jnp.bfloat16
WHOLE = pl.BlockSpec(memory_space=pltpu.VMEM)
SCALARS = pl.BlockSpec(memory_space=pltpu.SMEM)


def dot(a, b, dims):
    return lax.dot_general(a, b, dims, preferred_element_type=f32)


def pick_kernel(idx_ref, *refs):
    *pieces, out_ref, held = refs
    at = 0
    rows = out_ref.shape[1]
    for piece in pieces:
        for k in range(piece.shape[0] // rows):
            held[at] = piece[k * rows : (k + 1) * rows]
            at += 1
    for i in range(out_ref.shape[0]):
        out_ref[i] = held[idx_ref[i]]


def fold_kernel(idx_ref, terms_ref, out_ref, total):
    total[...] = jnp.zeros_like(total)
    count = terms_ref.shape[0] * terms_ref.shape[1]
    for i in range(count):
        p = idx_ref[i]
        total[p] = total[p] + terms_ref[i // 2, i % 2].astype(f32)
    out_ref[...] = total[...].astype(out_ref.dtype)


def attn_kernel(
    len_ref, q_ref, do_ref, kr_ref, vr_ref, kp_ref, vp_ref,
    o_ref, dq_ref, dkr_ref, dvr_ref, dp_ref,
    p_s, ds_s, g_s, ka, va,
):
    D = HEAD_SIZE
    heads = q_ref.shape[2] // D
    prompt_len = kp_ref.shape[0] * kp_ref.shape[2]
    r, g = pl.program_id(0), pl.program_id(1)
    n = len_ref[r]
    ka[:prompt_len] = kp_ref[...].reshape(prompt_len, D)
    ka[prompt_len:] = kr_ref[0]
    va[:prompt_len] = vp_ref[...].reshape(prompt_len, D)
    va[prompt_len:] = vr_ref[0]
    row = lax.broadcasted_iota(jnp.int32, (HALF, HALF), 0)
    col = lax.broadcasted_iota(jnp.int32, (HALF, HALF), 1)
    tri = col <= row
    rid = lax.broadcasted_iota(jnp.int32, (HALF, 1), 0)
    for half in range(2):
        j = prompt_len + HALF * (half + 1)
        rows = slice(half * HALF, (half + 1) * HALF)
        valid = (rid + half * HALF < n).astype(f32)
        for h in range(heads):
            cols = slice(h * D, (h + 1) * D)
            s = dot(q_ref[0, rows, cols], ka[:j], NT)
            s = jnp.concatenate([s[:, : j - HALF], jnp.where(tri, s[:, j - HALF :], -jnp.inf)], 1)
            m = jnp.max(s, 1, keepdims=True)
            p = jnp.exp2((s - m) * SCALE_LOG2)
            inv = valid / jnp.sum(p, 1, keepdims=True)
            pb = p.astype(bf16)
            ob = (dot(pb, va[:j], NN) * inv).astype(bf16)
            o_ref[0, rows, cols] = ob
            gh = (do_ref[0, rows, cols].astype(f32) * inv).astype(bf16)
            delta = jnp.sum(gh.astype(f32) * ob.astype(f32), 1, keepdims=True)
            ds = (p * (dot(gh, va[:j], NT) - delta)).astype(bf16)
            dq_ref[0, rows, cols] = (dot(ds, ka[:j], NN) * SCALE).astype(bf16)
            stack = slice(h * HALF, (h + 1) * HALF)
            p_s[half, stack, :j] = pb
            ds_s[half, stack, :j] = ds
            g_s[half, stack] = gh

    def stacked_queries(half):
        rows = slice(half * HALF, (half + 1) * HALF)
        return jnp.concatenate([q_ref[0, rows, h * D : (h + 1) * D] for h in range(heads)], 0)

    j0 = prompt_len + HALF
    dv1 = dot(p_s[1], g_s[1], TN)
    dv0 = dot(p_s[0, :, :j0], g_s[0], TN)
    dk1 = dot(ds_s[1], stacked_queries(1), TN)
    dk0 = dot(ds_s[0, :, :j0], stacked_queries(0), TN)
    dv = dv1[:j0] + dv0
    dk = (dk1[:j0] + dk0) * SCALE
    pieces = (dp_ref.shape[0], dp_ref.shape[2], D)
    kv_heads = dp_ref.shape[3] // (2 * D)
    dp_ref[:, 0, :, pl.ds(pl.multiple_of(g * D, D), D)] = dk[:prompt_len].astype(bf16).reshape(pieces)
    dp_ref[:, 0, :, pl.ds(pl.multiple_of((g + kv_heads) * D, D), D)] = (
        dv[:prompt_len].astype(bf16).reshape(pieces)
    )
    dkr_ref[0, :HALF] = dk[prompt_len:].astype(bf16)
    dkr_ref[0, HALF:] = (dk1[j0:] * SCALE).astype(bf16)
    dvr_ref[0, :HALF] = dv[prompt_len:].astype(bf16)
    dvr_ref[0, HALF:] = dv1[j0:].astype(bf16)


def attend(lengths, queries, out_grad, resp_keys, resp_values, prompt_kv):
    D = HEAD_SIZE
    count, token_rows, width = queries.shape
    kv_heads = resp_keys.shape[2] // D
    head_width = width // kv_heads
    blocks, _, block_rows, kv_width = prompt_kv.shape
    keys = blocks * block_rows + token_rows
    stack = head_width // D * HALF

    def block(w):
        return pl.BlockSpec((1, token_rows, w), lambda r, g: (r, 0, g))

    pk = pl.BlockSpec((blocks, 1, block_rows, D), lambda r, g: (0, r, 0, g))
    pv = pl.BlockSpec((blocks, 1, block_rows, D), lambda r, g: (0, r, 0, kv_heads + g))
    dp = pl.BlockSpec((blocks, 1, block_rows, kv_width), lambda r, g: (0, r, 0, 0))
    sds = jax.ShapeDtypeStruct
    return pl.pallas_call(
        attn_kernel,
        grid=(count, kv_heads),
        in_specs=[SCALARS, block(head_width), block(head_width), block(D), block(D), pk, pv],
        out_specs=[block(head_width), block(head_width), block(D), block(D), dp],
        out_shape=[
            sds(queries.shape, bf16),
            sds(queries.shape, bf16),
            sds(resp_keys.shape, bf16),
            sds(resp_keys.shape, bf16),
            sds(prompt_kv.shape, bf16),
        ],
        scratch_shapes=[
            pltpu.VMEM((2, stack, keys), bf16),
            pltpu.VMEM((2, stack, keys), bf16),
            pltpu.VMEM((2, stack, D), bf16),
            pltpu.VMEM((keys, D), bf16),
            pltpu.VMEM((keys, D), bf16),
        ],
        compiler_params=pltpu.CompilerParams(
            vmem_limit_bytes=48 * 2**20, dimension_semantics=("arbitrary", "arbitrary")
        ),
        name="attn",
    )(lengths, queries, out_grad, resp_keys, resp_values, prompt_kv, prompt_kv)


def local(
    planes,
    queries,
    resp_keys,
    response_values,
    prompt_key_rows,
    prompt_value_rows,
    out_grad,
    group_list,
    lengths,
):
    dp = lax.axis_size("dp")
    per_plane = dp // planes
    count = queries.shape[0]
    me = lax.axis_index("dp")
    plane = me // per_plane
    lanes = [[p * per_plane + j for j in range(per_plane)] for p in range(planes)]
    columns = [[p * per_plane + j for p in range(planes)] for j in range(per_plane)]

    def shift(v, k):
        pairs = [(i, (i + k * per_plane) % dp) for i in range(dp)]
        return lax.ppermute(v, "dp", pairs)

    ids = plane * (per_plane * count) + jnp.arange(per_plane * count, dtype=jnp.int32)
    member = (group_list[:, :, None] == ids[None, None, :]).astype(jnp.int32)
    prompt_of = jnp.sum(
        jnp.arange(planes, dtype=jnp.int32)[:, None] * jnp.sum(member, axis=1), axis=0
    )

    mine = jnp.concatenate([prompt_key_rows, prompt_value_rows], 1)
    rows, kv_width = mine.shape
    half_turn = shift(mine, 4)
    plus2, minus2 = shift(mine, 2), shift(mine, -2)
    both = jnp.concatenate([mine, half_turn], 0)
    plus1, minus1 = shift(both, 1), shift(both, -1)
    place = jnp.array([0, 2, 6, 5, 1, 3, 7, 4], jnp.int32)
    idx = place[(plane - prompt_of) % planes]
    picked = pl.pallas_call(
        pick_kernel,
        in_specs=[SCALARS] + [WHOLE] * 5,
        out_specs=WHOLE,
        out_shape=jax.ShapeDtypeStruct((per_plane * count, rows, kv_width), bf16),
        scratch_shapes=[pltpu.VMEM((planes, rows, kv_width), bf16)],
        name="pick",
    )(idx, both, plus1, minus1, plus2, minus2)
    picked = picked.reshape(per_plane, count, rows, kv_width)
    prompt_kv = lax.all_to_all(picked, "dp", 0, 0, axis_index_groups=lanes)

    attn_out, grad_q, grad_k, grad_v, grad_prompt = attend(
        lengths, queries, out_grad, resp_keys, response_values, prompt_kv
    )

    back = lax.all_to_all(grad_prompt, "dp", 0, 0, axis_index_groups=lanes)
    folded = pl.pallas_call(
        fold_kernel,
        in_specs=[SCALARS, WHOLE],
        out_specs=WHOLE,
        out_shape=jax.ShapeDtypeStruct((planes, rows, kv_width), bf16),
        scratch_shapes=[pltpu.VMEM((planes, rows, kv_width), f32)],
        name="fold",
    )(prompt_of, back)
    terms = lax.all_to_all(folded, "dp", 0, 0, axis_index_groups=columns)
    total = jnp.sum(terms.astype(f32), axis=0).astype(bf16)
    key_width = prompt_key_rows.shape[1]
    return attn_out, grad_q, grad_k, grad_v, total[:, :key_width], total[:, key_width:]


def solution(mesh):
    in_specs = (
        P("dp", None, "tensor"),
        P("dp", None, "tensor"),
        P("dp", None, "tensor"),
        P("dp", "tensor"),
        P("dp", "tensor"),
        P("dp", None, "tensor"),
        P(),
        P("dp"),
    )
    out_specs = (
        P("dp", None, "tensor"),
        P("dp", None, "tensor"),
        P("dp", None, "tensor"),
        P("dp", None, "tensor"),
        P("dp", "tensor"),
        P("dp", "tensor"),
    )

    def step(*args):
        planes = args[6].shape[0]
        return jax.shard_map(
            functools.partial(local, planes),
            mesh=mesh,
            in_specs=in_specs,
            out_specs=out_specs,
            check_vma=False,
        )(*args)

    return step
```

```python
import functools
import math

import jax
import jax.numpy as jnp
from jax import lax
from jax.experimental import pallas as pl
from jax.experimental.pallas import tpu as pltpu
from jax.sharding import PartitionSpec as P

HEAD_SIZE = 128
SCALE = HEAD_SIZE**-0.5
SCALE_LOG2 = SCALE * math.log2(math.e)
HALF = 128
CHUNK = 256
LEAD = 4
NT = (((1,), (1,)), ((), ()))
NN = (((1,), (0,)), ((), ()))
TN = (((0,), (0,)), ((), ()))
f32 = jnp.float32
bf16 = jnp.bfloat16
WHOLE = pl.BlockSpec(memory_space=pltpu.VMEM)
ANY = pl.BlockSpec(memory_space=pl.ANY)
SCALARS = pl.BlockSpec(memory_space=pltpu.SMEM)


def dot(a, b, dims):
    return lax.dot_general(a, b, dims, preferred_element_type=f32)


def pick_kernel(idx_ref, *refs):
    *pieces, out_ref, held, in_sems, out_sems = refs
    rows = out_ref.shape[1]
    copies = []
    at = 0
    for n, piece in enumerate(pieces):
        k = piece.shape[0] // rows
        for m in range(k):
            copies.append(
                pltpu.make_async_copy(
                    piece.at[pl.ds(m * rows, rows)], held.at[at + m], in_sems.at[at + m]
                )
            )
        at += k
    for c in copies:
        c.start()
    for c in copies:
        c.wait()
    copies = [
        pltpu.make_async_copy(held.at[idx_ref[i]], out_ref.at[i], out_sems.at[i])
        for i in range(out_ref.shape[0])
    ]
    for c in copies:
        c.start()
    for c in copies:
        c.wait()


def fold_kernel(idx_ref, terms_ref, up_ref, down_ref, up2_ref, down2_ref, keep_ref, total):
    total[...] = jnp.zeros_like(total)
    per = terms_ref.shape[1]
    for i in range(terms_ref.shape[0] * per):
        d = idx_ref[i]
        total[d] = total[d] + terms_ref[i // per, i % per].astype(f32)
    up_ref[0], up_ref[1] = total[1].astype(bf16), total[5].astype(bf16)
    down_ref[0], down_ref[1] = total[7].astype(bf16), total[3].astype(bf16)
    up2_ref[...] = total[2].astype(bf16)
    down2_ref[...] = total[6].astype(bf16)
    keep_ref[0], keep_ref[1] = total[0], total[4]


def attn_kernel(
    len_ref, q_ref, do_ref, kr_ref, vr_ref, kp_ref, vp_ref,
    o_ref, dq_ref, dkr_ref, dvr_ref, dp_ref,
    p_s, ds_s, g_s, q_s, ka, va, dk_s, dv_s,
):
    D = HEAD_SIZE
    heads = q_ref.shape[2] // D
    prompt_len = kp_ref.shape[0] * kp_ref.shape[2]
    n = len_ref[pl.program_id(0)]
    ka[:prompt_len] = kp_ref[...].reshape(prompt_len, D)
    ka[prompt_len:] = kr_ref[0]
    va[:prompt_len] = vp_ref[...].reshape(prompt_len, D)
    va[prompt_len:] = vr_ref[0]
    row = lax.broadcasted_iota(jnp.int32, (HALF, HALF), 0)
    col = lax.broadcasted_iota(jnp.int32, (HALF, HALF), 1)
    tri = jnp.concatenate([col <= row] * heads, 0)
    rid = lax.broadcasted_iota(jnp.int32, (HALF, 1), 0)
    first = prompt_len + HALF

    def chain(half):
        j = first + HALF * half
        rows = slice(half * HALF, (half + 1) * HALF)
        head_cols = [slice(h * D, (h + 1) * D) for h in range(heads)]
        head_rows = [slice(h * HALF, (h + 1) * HALF) for h in range(heads)]
        q_s[half] = jnp.concatenate([q_ref[0, rows, c] for c in head_cols], 0)
        chunks = [(a, min(a + CHUNK, j)) for a in range(0, j, CHUNK)]
        top, kept = None, []
        for a, b in chunks:
            s = dot(q_s[half], ka[a:b], NT)
            if b == j:
                last = jnp.where(tri, s[:, b - a - HALF :], -jnp.inf)
                s = jnp.concatenate([s[:, : b - a - HALF], last], 1) if b - a > HALF else last
            kept.append(s)
            for k in range(0, b - a, HALF):
                part = s[:, k : k + HALF]
                top = part if top is None else jnp.maximum(top, part)
            yield
        m = jnp.max(top, 1, keepdims=True) * SCALE_LOG2
        yield
        norm, out = None, None
        for n_chunk, (a, b) in enumerate(chunks):
            p = jnp.exp2(kept[n_chunk] * SCALE_LOG2 - m)
            kept[n_chunk] = p
            for k in range(0, b - a, HALF):
                part = p[:, k : k + HALF]
                norm = part if norm is None else norm + part
            pb = p.astype(bf16)
            p_s[half, :, a:b] = pb
            t = dot(pb, va[a:b], NN)
            out = t if out is None else out + t
            yield
        valid = jnp.concatenate([(rid + half * HALF < n).astype(f32)] * heads, 0)
        inv = valid / jnp.sum(norm, 1, keepdims=True)
        ob = (out * inv).astype(bf16)
        for c, s in zip(head_cols, head_rows):
            o_ref[0, rows, c] = ob[s]
        gh = jnp.concatenate([do_ref[0, rows, c] for c in head_cols], 0)
        gh = (gh.astype(f32) * inv).astype(bf16)
        g_s[half] = gh
        delta = jnp.sum(gh.astype(f32) * ob.astype(f32), 1, keepdims=True)
        yield
        grad = None
        for n_chunk, (a, b) in enumerate(chunks):
            x = dot(g_s[half], va[a:b], NT)
            ds = (kept[n_chunk] * (x - delta)).astype(bf16)
            ds_s[half, :, a:b] = ds
            t = dot(ds, ka[a:b], NN)
            grad = t if grad is None else grad + t
            yield
        grad = (grad * SCALE).astype(bf16)
        for c, s in zip(head_cols, head_rows):
            dq_ref[0, rows, c] = grad[s]
        for a, b in chunks:
            dv = dot(p_s[half, :, a:b], g_s[half], TN)
            dk = dot(ds_s[half, :, a:b], q_s[half], TN)
            if half == 0:
                dv_s[a:b], dk_s[a:b] = dv, dk
            else:
                e, f = min(b, first), max(a, first)
                if e > a:
                    dv_s[a:e] += dv[: e - a]
                    dk_s[a:e] += dk[: e - a]
                if b > f:
                    dv_s[f:b], dk_s[f:b] = dv[f - a :], dk[f - a :]
            yield

    lead, follow = chain(0), chain(1)
    for _ in range(LEAD):
        next(lead)
    live = [lead, follow]
    while live:
        for c in list(live):
            if next(c, c) is c:
                live.remove(c)
    dk = dk_s[...] * SCALE
    blocks, block_rows = kp_ref.shape[0], kp_ref.shape[2]
    pieces = (blocks, block_rows, D)
    cols = pl.ds(pl.multiple_of(pl.program_id(1) * D, D), D)
    dp_ref[:, 0, :block_rows, cols] = dk[:prompt_len].astype(bf16).reshape(pieces)
    dp_ref[:, 0, block_rows:, cols] = dv_s[:prompt_len].astype(bf16).reshape(pieces)
    dkr_ref[0] = dk[prompt_len:].astype(bf16)
    dvr_ref[0] = dv_s[prompt_len:].astype(bf16)


def attend(lengths, queries, out_grad, resp_keys, resp_values, prompt_kv):
    D = HEAD_SIZE
    count, token_rows, width = queries.shape
    kv_heads = resp_keys.shape[2] // D
    head_width = width // kv_heads
    blocks, _, both_rows, _ = prompt_kv.shape
    rows = both_rows // 2
    keys = blocks * rows + token_rows
    stack = head_width // D * HALF

    def block(w):
        return pl.BlockSpec((1, token_rows, w), lambda r, g: (r, 0, g))

    pk = pl.BlockSpec((blocks, 1, rows, D), lambda r, g: (0, r, 0, g))
    pv = pl.BlockSpec((blocks, 1, rows, D), lambda r, g: (0, r, 1, g))
    dp = pl.BlockSpec((blocks, 1, both_rows, kv_heads * D), lambda r, g: (0, r, 0, 0))
    sds = jax.ShapeDtypeStruct
    return pl.pallas_call(
        attn_kernel,
        grid=(count, kv_heads),
        in_specs=[SCALARS, block(head_width), block(head_width), block(D), block(D), pk, pv],
        out_specs=[block(head_width), block(head_width), block(D), block(D), dp],
        out_shape=[
            sds(queries.shape, bf16),
            sds(queries.shape, bf16),
            sds(resp_keys.shape, bf16),
            sds(resp_keys.shape, bf16),
            sds(prompt_kv.shape, bf16),
        ],
        scratch_shapes=[
            pltpu.VMEM((2, stack, keys), bf16),
            pltpu.VMEM((2, stack, keys), bf16),
            pltpu.VMEM((2, stack, D), bf16),
            pltpu.VMEM((2, stack, D), bf16),
            pltpu.VMEM((keys, D), bf16),
            pltpu.VMEM((keys, D), bf16),
            pltpu.VMEM((keys, D), f32),
            pltpu.VMEM((keys, D), f32),
        ],
        compiler_params=pltpu.CompilerParams(
            vmem_limit_bytes=48 * 2**20, dimension_semantics=("arbitrary", "arbitrary")
        ),
        name="attn",
    )(lengths, queries, out_grad, resp_keys, resp_values, prompt_kv, prompt_kv)


def local(
    planes,
    queries,
    resp_keys,
    response_values,
    prompt_key_rows,
    prompt_value_rows,
    out_grad,
    group_list,
    lengths,
):
    dp = lax.axis_size("dp")
    per_plane = dp // planes
    count = queries.shape[0]
    me = lax.axis_index("dp")
    plane = me // per_plane
    lanes = [[p * per_plane + j for j in range(per_plane)] for p in range(planes)]

    def shift(v, k):
        pairs = [(i, (i + k * per_plane) % dp) for i in range(dp)]
        return lax.ppermute(v, "dp", pairs)

    ids = plane * (per_plane * count) + jnp.arange(per_plane * count, dtype=jnp.int32)
    member = group_list[:, :, None] == ids[None, None, :]
    above = (jnp.arange(planes, dtype=jnp.int32) - plane) % planes

    def by_prompt(value):
        return jnp.sum(jnp.where(member, value[:, None, None], 0), axis=(0, 1))

    mine = jnp.concatenate([prompt_key_rows, prompt_value_rows], 0)
    rows, kv_width = mine.shape
    half_turn = shift(mine, 4)
    from2, from6 = shift(mine, -2), shift(mine, 2)
    both = jnp.concatenate([mine, half_turn], 0)
    from1, from7 = shift(both, -1), shift(both, 1)
    order = [0, 4, 1, 5, 7, 3, 2, 6]
    place = sum(jnp.where(above == d, at, 0) for at, d in enumerate(order))
    picked = pl.pallas_call(
        pick_kernel,
        in_specs=[SCALARS] + [ANY] * 5,
        out_specs=ANY,
        out_shape=jax.ShapeDtypeStruct((per_plane * count, rows, kv_width), bf16),
        scratch_shapes=[
            pltpu.VMEM((planes, rows, kv_width), bf16),
            pltpu.SemaphoreType.DMA((planes,)),
            pltpu.SemaphoreType.DMA((per_plane * count,)),
        ],
        name="pick",
    )(by_prompt(place), both, from1, from7, from2, from6)
    picked = picked.reshape(per_plane, count, rows, kv_width)
    prompt_kv = lax.all_to_all(picked, "dp", 0, 0, axis_index_groups=lanes)

    attn_out, grad_q, grad_k, grad_v, grad_prompt = attend(
        lengths, queries, out_grad, resp_keys, response_values, prompt_kv
    )

    back = lax.all_to_all(grad_prompt, "dp", 0, 0, axis_index_groups=lanes)
    sds = jax.ShapeDtypeStruct
    up, down, up2, down2, keep = pl.pallas_call(
        fold_kernel,
        in_specs=[SCALARS, WHOLE],
        out_specs=[WHOLE] * 5,
        out_shape=[
            sds((2, rows, kv_width), bf16),
            sds((2, rows, kv_width), bf16),
            sds((rows, kv_width), bf16),
            sds((rows, kv_width), bf16),
            sds((2, rows, kv_width), f32),
        ],
        scratch_shapes=[pltpu.VMEM((planes, rows, kv_width), f32)],
        name="fold",
    )(by_prompt(above), back)
    up, down = shift(up, 1), shift(down, -1)
    up2, down2 = shift(up2, 2), shift(down2, -2)
    far = shift((keep[1] + up[1].astype(f32) + down[1].astype(f32)).astype(bf16), 4)
    near = keep[0] + up[0].astype(f32) + down[0].astype(f32)
    total = near + up2.astype(f32) + down2.astype(f32) + far.astype(f32)
    total = total.astype(bf16)
    key_rows = prompt_key_rows.shape[0]
    return attn_out, grad_q, grad_k, grad_v, total[:key_rows], total[key_rows:]


def solution(mesh):
    in_specs = (
        P("dp", None, "tensor"),
        P("dp", None, "tensor"),
        P("dp", None, "tensor"),
        P("dp", "tensor"),
        P("dp", "tensor"),
        P("dp", None, "tensor"),
        P(),
        P("dp"),
    )
    out_specs = (
        P("dp", None, "tensor"),
        P("dp", None, "tensor"),
        P("dp", None, "tensor"),
        P("dp", None, "tensor"),
        P("dp", "tensor"),
        P("dp", "tensor"),
    )

    def step(*args):
        planes = args[6].shape[0]
        return jax.shard_map(
            functools.partial(local, planes),
            mesh=mesh,
            in_specs=in_specs,
            out_specs=out_specs,
            check_vma=False,
        )(*args)

    return step
```

```python
import functools
import math

import jax
import jax.numpy as jnp
from jax import lax
from jax.experimental import pallas as pl
from jax.experimental.pallas import tpu as pltpu
from jax.sharding import PartitionSpec as P

HEAD_SIZE = 128
SCALE = HEAD_SIZE**-0.5
SCALE_LOG2 = SCALE * math.log2(math.e)
HALF = 128
CHUNK = 256
LEAD = 4
NT = (((1,), (1,)), ((), ()))
NN = (((1,), (0,)), ((), ()))
TN = (((0,), (0,)), ((), ()))
f32 = jnp.float32
bf16 = jnp.bfloat16
WHOLE = pl.BlockSpec(memory_space=pltpu.VMEM)
ANY = pl.BlockSpec(memory_space=pl.ANY)
SCALARS = pl.BlockSpec(memory_space=pltpu.SMEM)


def dot(a, b, dims):
    return lax.dot_general(a, b, dims, preferred_element_type=f32)


def pick_kernel(idx_ref, own_ref, partner_ref, *refs):
    *outs, sems = refs
    copies = []
    for i, out in enumerate(outs):
        block = idx_ref[i]
        for n, piece in enumerate((own_ref, partner_ref)):
            copies.append(
                pltpu.make_async_copy(piece.at[block], out.at[n], sems.at[2 * i + n])
            )
    for c in copies:
        c.start()
    for c in copies:
        c.wait()


def fold_kernel(idx_ref, *refs):
    *terms, up_ref, down_ref, up2_ref, down2_ref, keep_ref, total = refs
    total[...] = jnp.zeros_like(total)
    at = 0
    for term in terms:
        for k in range(term.shape[0]):
            d = idx_ref[at]
            total[d] = total[d] + term[k].astype(f32)
            at += 1
    up_ref[0], up_ref[1] = total[1].astype(bf16), total[5].astype(bf16)
    down_ref[0], down_ref[1] = total[7].astype(bf16), total[3].astype(bf16)
    up2_ref[...] = total[2].astype(bf16)
    down2_ref[...] = total[6].astype(bf16)
    keep_ref[0], keep_ref[1] = total[0], total[4]


def attn_kernel(slot, parts, len_ref, q_ref, do_ref, kr_ref, vr_ref, *refs):
    kp_refs, vp_refs, refs = refs[:parts], refs[parts : 2 * parts], refs[2 * parts :]
    refs = refs[0 if slot == 0 else 4 :]
    o_ref, dq_ref, dkr_ref, dvr_ref, *refs = refs
    dp_refs, refs = refs[:parts], refs[parts:]
    p_s, ds_s, g_s, q_s, ka, va, dk_s, dv_s = refs
    D = HEAD_SIZE
    heads = q_ref.shape[2] // D
    block_rows = kp_refs[0].shape[1]
    part_rows = kp_refs[0].shape[0] * block_rows
    prompt_len = parts * part_rows
    n = len_ref[slot]
    for k in range(parts):
        rows = slice(k * part_rows, (k + 1) * part_rows)
        ka[rows] = kp_refs[k][...].reshape(part_rows, D)
        va[rows] = vp_refs[k][...].reshape(part_rows, D)
    ka[prompt_len:] = kr_ref[0]
    va[prompt_len:] = vr_ref[0]
    row = lax.broadcasted_iota(jnp.int32, (HALF, HALF), 0)
    col = lax.broadcasted_iota(jnp.int32, (HALF, HALF), 1)
    tri = jnp.concatenate([col <= row] * heads, 0)
    rid = lax.broadcasted_iota(jnp.int32, (HALF, 1), 0)
    first = prompt_len + HALF

    def chain(half):
        j = first + HALF * half
        rows = slice(half * HALF, (half + 1) * HALF)
        head_cols = [slice(h * D, (h + 1) * D) for h in range(heads)]
        head_rows = [slice(h * HALF, (h + 1) * HALF) for h in range(heads)]
        q_s[half] = jnp.concatenate([q_ref[0, rows, c] for c in head_cols], 0)
        chunks = [(a, min(a + CHUNK, j)) for a in range(0, j, CHUNK)]
        top, kept = None, []
        for a, b in chunks:
            s = dot(q_s[half], ka[a:b], NT)
            if b == j:
                last = jnp.where(tri, s[:, b - a - HALF :], -jnp.inf)
                s = jnp.concatenate([s[:, : b - a - HALF], last], 1) if b - a > HALF else last
            kept.append(s)
            for k in range(0, b - a, HALF):
                part = s[:, k : k + HALF]
                top = part if top is None else jnp.maximum(top, part)
            yield
        m = jnp.max(top, 1, keepdims=True) * SCALE_LOG2
        yield
        norm, out = None, None
        for n_chunk, (a, b) in enumerate(chunks):
            p = jnp.exp2(kept[n_chunk] * SCALE_LOG2 - m)
            kept[n_chunk] = p
            for k in range(0, b - a, HALF):
                part = p[:, k : k + HALF]
                norm = part if norm is None else norm + part
            pb = p.astype(bf16)
            p_s[half, :, a:b] = pb
            t = dot(pb, va[a:b], NN)
            out = t if out is None else out + t
            yield
        valid = jnp.concatenate([(rid + half * HALF < n).astype(f32)] * heads, 0)
        inv = valid / jnp.sum(norm, 1, keepdims=True)
        ob = (out * inv).astype(bf16)
        for c, s in zip(head_cols, head_rows):
            o_ref[0, rows, c] = ob[s]
        gh = jnp.concatenate([do_ref[0, rows, c] for c in head_cols], 0)
        gh = (gh.astype(f32) * inv).astype(bf16)
        g_s[half] = gh
        delta = jnp.sum(gh.astype(f32) * ob.astype(f32), 1, keepdims=True)
        yield
        grad = None
        for n_chunk, (a, b) in enumerate(chunks):
            x = dot(g_s[half], va[a:b], NT)
            ds = (kept[n_chunk] * (x - delta)).astype(bf16)
            ds_s[half, :, a:b] = ds
            t = dot(ds, ka[a:b], NN)
            grad = t if grad is None else grad + t
            yield
        grad = (grad * SCALE).astype(bf16)
        for c, s in zip(head_cols, head_rows):
            dq_ref[0, rows, c] = grad[s]
        for a, b in chunks:
            dv = dot(p_s[half, :, a:b], g_s[half], TN)
            dk = dot(ds_s[half, :, a:b], q_s[half], TN)
            if half == 0:
                dv_s[a:b], dk_s[a:b] = dv, dk
            else:
                e, f = min(b, first), max(a, first)
                if e > a:
                    dv_s[a:e] += dv[: e - a]
                    dk_s[a:e] += dk[: e - a]
                if b > f:
                    dv_s[f:b], dk_s[f:b] = dv[f - a :], dk[f - a :]
            yield

    lead, follow = chain(0), chain(1)
    for _ in range(LEAD):
        next(lead)
    live = [lead, follow]
    while live:
        for c in list(live):
            if next(c, c) is c:
                live.remove(c)
    dk = dk_s[...] * SCALE
    cols = pl.ds(pl.multiple_of(pl.program_id(0) * D, D), D)
    for k in range(parts):
        rows = slice(k * part_rows, (k + 1) * part_rows)
        pieces = kp_refs[k].shape
        dp_refs[k][:, :block_rows, cols] = dk[rows].astype(bf16).reshape(pieces)
        dp_refs[k][:, block_rows:, cols] = dv_s[rows].astype(bf16).reshape(pieces)
    dkr_ref[0] = dk[prompt_len:].astype(bf16)
    dvr_ref[0] = dv_s[prompt_len:].astype(bf16)


def attend(slot, lengths, queries, out_grad, resp_keys, resp_values, prompt_parts, done):
    D = HEAD_SIZE
    _, token_rows, width = queries.shape
    kv_heads = resp_keys.shape[2] // D
    head_width = width // kv_heads
    parts = len(prompt_parts)
    cores, both_rows, kv_width = prompt_parts[0].shape
    rows = both_rows // 2
    keys = parts * cores * rows + token_rows
    stack = head_width // D * HALF

    def block(w):
        return pl.BlockSpec((1, token_rows, w), lambda g: (slot, 0, g))

    pk = pl.BlockSpec((cores, rows, D), lambda g: (0, 0, g))
    pv = pl.BlockSpec((cores, rows, D), lambda g: (0, 1, g))
    dp = pl.BlockSpec((cores, both_rows, kv_width), lambda g: (0, 0, 0))
    sds = jax.ShapeDtypeStruct
    like = (queries, queries, resp_keys, resp_keys)
    outs = pl.pallas_call(
        functools.partial(attn_kernel, slot, parts),
        grid=(kv_heads,),
        in_specs=[SCALARS, block(head_width), block(head_width), block(D), block(D)]
        + [pk] * parts
        + [pv] * parts
        + [ANY] * len(done),
        out_specs=[block(head_width), block(head_width), block(D), block(D)] + [dp] * parts,
        out_shape=[sds(x.shape, bf16) for x in like] + [sds(prompt_parts[0].shape, bf16)] * parts,
        input_output_aliases={5 + 2 * parts + i: i for i in range(len(done))},
        scratch_shapes=[
            pltpu.VMEM((2, stack, keys), bf16),
            pltpu.VMEM((2, stack, keys), bf16),
            pltpu.VMEM((2, stack, D), bf16),
            pltpu.VMEM((2, stack, D), bf16),
            pltpu.VMEM((keys, D), bf16),
            pltpu.VMEM((keys, D), bf16),
            pltpu.VMEM((keys, D), f32),
            pltpu.VMEM((keys, D), f32),
        ],
        compiler_params=pltpu.CompilerParams(
            vmem_limit_bytes=36 * 2**20, dimension_semantics=("arbitrary",)
        ),
        cost_estimate=pl.CostEstimate(
            flops=12 * token_rows * keys * width, bytes_accessed=8 * token_rows * width, transcendentals=0
        ),
        name="attn",
    )(lengths, queries, out_grad, resp_keys, resp_values, *prompt_parts, *prompt_parts, *done)
    return outs[:4], outs[4:]


def local(
    planes,
    queries,
    resp_keys,
    response_values,
    prompt_key_rows,
    prompt_value_rows,
    out_grad,
    group_list,
    lengths,
):
    dp = lax.axis_size("dp")
    per_plane = dp // planes
    chips = per_plane // 2
    count = queries.shape[0]
    me = lax.axis_index("dp")
    plane, chip, core = me // per_plane, me % per_plane // 2, me % 2

    def shift(v, k):
        return lax.ppermute(v, "dp", [(i, (i + k * per_plane) % dp) for i in range(dp)])

    def turn(v, k):
        pairs = [
            (i, i // per_plane * per_plane + (i % per_plane + 2 * k) % per_plane) for i in range(dp)
        ]
        return lax.ppermute(v, "dp", pairs)

    def swap(v):
        return lax.ppermute(v, "dp", [(i, i ^ 1) for i in range(dp)])

    there = (chip + jnp.arange(chips, dtype=jnp.int32)) % chips
    cores = jnp.stack([core, 1 - core])
    device = (plane * chips + there[None, :]) * 2 + cores[:, None]
    ids = (device[:, :, None] * count + jnp.arange(count, dtype=jnp.int32)).reshape(-1)
    member = group_list[:, :, None] == ids[None, None, :]
    above = (jnp.arange(planes, dtype=jnp.int32) - plane) % planes

    def by_prompt(value):
        return jnp.sum(jnp.where(member, value[:, None, None], 0), axis=(0, 1))

    mine = jnp.concatenate([prompt_key_rows, prompt_value_rows], 0)
    rows, kv_width = mine.shape
    half_turn = shift(mine, 4)
    from2, from6 = shift(mine, -2), shift(mine, 2)
    both = jnp.concatenate([mine, half_turn], 0)
    from1, from7 = shift(both, -1), shift(both, 1)
    order = [0, 4, 1, 5, 7, 3, 2, 6]
    place = sum(jnp.where(above == d, at, 0) for at, d in enumerate(order))
    pieces = jnp.concatenate([both, from1, from7, from2, from6], 0).reshape(planes, rows, kv_width)
    partner = swap(pieces)
    sends = chips * count
    picked = pl.pallas_call(
        pick_kernel,
        in_specs=[SCALARS, ANY, ANY],
        out_specs=[ANY] * sends,
        out_shape=[jax.ShapeDtypeStruct((2, rows, kv_width), bf16)] * sends,
        scratch_shapes=[pltpu.SemaphoreType.DMA((2 * sends,))],
        compiler_params=pltpu.CompilerParams(vmem_limit_bytes=2**20),
        name="pick",
    )(by_prompt(place), pieces, partner)
    prompts = [
        [picked[r]] + [turn(picked[k * count + r], k) for k in range(1, chips)]
        for r in range(count)
    ]

    written, terms, partner_terms = [], [], []
    for r in range(count):
        written, grads = attend(
            r, lengths, queries, out_grad, resp_keys, response_values, prompts[r], written
        )
        back = [grads[0]] + [turn(grads[k], -k) for k in range(1, chips)]
        terms.append(jnp.stack([g[0] for g in back]))
        partner_terms.append(swap(jnp.stack([g[1] for g in back])))
    attn_out, grad_q, grad_k, grad_v = written

    by_slot = by_prompt(above).reshape(2, chips, count).transpose(0, 2, 1).reshape(-1)
    sds = jax.ShapeDtypeStruct
    up, down, up2, down2, keep = pl.pallas_call(
        fold_kernel,
        in_specs=[SCALARS] + [WHOLE] * (2 * count),
        out_specs=[WHOLE] * 5,
        out_shape=[
            sds((2, rows, kv_width), bf16),
            sds((2, rows, kv_width), bf16),
            sds((rows, kv_width), bf16),
            sds((rows, kv_width), bf16),
            sds((2, rows, kv_width), f32),
        ],
        scratch_shapes=[pltpu.VMEM((planes, rows, kv_width), f32)],
        compiler_params=pltpu.CompilerParams(vmem_limit_bytes=8 * 2**20),
        name="fold",
    )(by_slot, *terms, *partner_terms)
    up, down = shift(up, 1), shift(down, -1)
    up2, down2 = shift(up2, 2), shift(down2, -2)
    far = shift((keep[1] + up[1].astype(f32) + down[1].astype(f32)).astype(bf16), 4)
    near = keep[0] + up[0].astype(f32) + down[0].astype(f32)
    total = near + up2.astype(f32) + down2.astype(f32) + far.astype(f32)
    total = total.astype(bf16)
    key_rows = prompt_key_rows.shape[0]
    return attn_out, grad_q, grad_k, grad_v, total[:key_rows], total[key_rows:]


def solution(mesh):
    in_specs = (
        P("dp", None, "tensor"),
        P("dp", None, "tensor"),
        P("dp", None, "tensor"),
        P("dp", "tensor"),
        P("dp", "tensor"),
        P("dp", None, "tensor"),
        P(),
        P("dp"),
    )
    out_specs = (
        P("dp", None, "tensor"),
        P("dp", None, "tensor"),
        P("dp", None, "tensor"),
        P("dp", None, "tensor"),
        P("dp", "tensor"),
        P("dp", "tensor"),
    )

    def step(*args):
        planes = args[6].shape[0]
        return jax.shard_map(
            functools.partial(local, planes),
            mesh=mesh,
            in_specs=in_specs,
            out_specs=out_specs,
            check_vma=False,
        )(*args)

    return step
```

```python
import functools
import math

import jax
import jax.numpy as jnp
from jax import lax
from jax.experimental import pallas as pl
from jax.experimental.pallas import tpu as pltpu
from jax.sharding import PartitionSpec as P

HEAD_SIZE = 128
SCALE = HEAD_SIZE**-0.5
SCALE_LOG2 = SCALE * math.log2(math.e)
HALF = 128
CHUNK = 256
LEAD = 3
ATTN_VMEM = 28 * 2**20
NT = (((1,), (1,)), ((), ()))
NN = (((1,), (0,)), ((), ()))
TN = (((0,), (0,)), ((), ()))
f32 = jnp.float32
bf16 = jnp.bfloat16
WHOLE = pl.BlockSpec(memory_space=pltpu.VMEM)
ANY = pl.BlockSpec(memory_space=pl.ANY)
HBM = pl.BlockSpec(memory_space=pltpu.HBM)
SCALARS = pl.BlockSpec(memory_space=pltpu.SMEM)


def dot(a, b, dims):
    return lax.dot_general(a, b, dims, preferred_element_type=f32)


def pick_kernel(idx_ref, own_ref, partner_ref, *outs):
    for i, out in enumerate(outs):
        block = idx_ref[i]
        out[0] = own_ref[block]
        out[1] = partner_ref[block]


def fold_kernel(idx_ref, *refs):
    *terms, up_ref, down_ref, up2_ref, down2_ref, keep_ref, total = refs
    total[...] = jnp.zeros_like(total)
    at = 0
    for term in terms:
        for k in range(term.shape[0]):
            d = idx_ref[at]
            total[d] = total[d] + term[k].astype(f32)
            at += 1
    up_ref[0], up_ref[1] = total[1].astype(bf16), total[5].astype(bf16)
    down_ref[0], down_ref[1] = total[7].astype(bf16), total[3].astype(bf16)
    up2_ref[...] = total[2].astype(bf16)
    down2_ref[...] = total[6].astype(bf16)
    keep_ref[0], keep_ref[1] = total[0], total[4]


def attn_kernel(slot, parts, len_ref, q_ref, do_ref, kr_ref, vr_ref, *refs):
    part_refs, refs = refs[:parts], refs[parts:]
    refs = refs[0 if slot == 0 else 4 :]
    o_ref, dq_ref, dkr_ref, dvr_ref, *refs = refs
    dp_refs, refs = refs[:parts], refs[parts:]
    p_s, ds_s, g_s, q_s, ka, va, dk_s, dv_s, do_s, do_sem = refs
    do_copy = pltpu.make_async_copy(do_ref.at[slot], do_s, do_sem)
    do_copy.start()
    arrived = []
    D = HEAD_SIZE
    kv_heads = kr_ref.shape[2] // D
    heads = q_ref.shape[2] // (D * kv_heads)
    cores, both_rows, _ = part_refs[0].shape
    block_rows = both_rows // 2
    part_rows = cores * block_rows
    prompt_len = parts * part_rows
    n = len_ref[slot]
    for g in range(kv_heads):
        cols = slice(g * D, (g + 1) * D)
        for k in range(parts):
            rows = slice(k * part_rows, (k + 1) * part_rows)
            ka[g, rows] = part_refs[k][:, :block_rows, cols].reshape(part_rows, D)
            va[g, rows] = part_refs[k][:, block_rows:, cols].reshape(part_rows, D)
        ka[g, prompt_len:] = kr_ref[slot, :, cols]
        va[g, prompt_len:] = vr_ref[slot, :, cols]
    row = lax.broadcasted_iota(jnp.int32, (HALF, HALF), 0)
    col = lax.broadcasted_iota(jnp.int32, (HALF, HALF), 1)
    tri = jnp.concatenate([col <= row] * heads, 0)
    rid = lax.broadcasted_iota(jnp.int32, (HALF, 1), 0)
    first = prompt_len + HALF

    def chain(g, half):
        u = 2 * g + half
        j = first + HALF * half
        rows = slice(half * HALF, (half + 1) * HALF)
        head_cols = [slice((g * heads + h) * D, (g * heads + h + 1) * D) for h in range(heads)]
        head_rows = [slice(h * HALF, (h + 1) * HALF) for h in range(heads)]
        q_s[u] = jnp.concatenate([q_ref[slot, rows, c] for c in head_cols], 0)
        chunks = [(a, min(a + CHUNK, j)) for a in range(0, j, CHUNK)]
        top, kept = None, []
        for a, b in chunks:
            s = dot(q_s[u], ka[g, a:b], NT)
            if b == j:
                last = jnp.where(tri, s[:, b - a - HALF :], -jnp.inf)
                s = jnp.concatenate([s[:, : b - a - HALF], last], 1) if b - a > HALF else last
            kept.append(s)
            for k in range(0, b - a, HALF):
                part = s[:, k : k + HALF]
                top = part if top is None else jnp.maximum(top, part)
            yield
        m = jnp.max(top, 1, keepdims=True) * SCALE_LOG2
        yield
        norm, out = None, None
        for i, (a, b) in enumerate(chunks):
            p = jnp.exp2(kept[i] * SCALE_LOG2 - m)
            kept[i] = p
            for k in range(0, b - a, HALF):
                part = p[:, k : k + HALF]
                norm = part if norm is None else norm + part
            pb = p.astype(bf16)
            p_s[u, :, a:b] = pb
            t = dot(pb, va[g, a:b], NN)
            out = t if out is None else out + t
            yield
        valid = jnp.concatenate([(rid + half * HALF < n).astype(f32)] * heads, 0)
        inv = valid / jnp.sum(norm, 1, keepdims=True)
        ob = (out * inv).astype(bf16)
        for c, s in zip(head_cols, head_rows):
            o_ref[0, rows, c] = ob[s]
        if not arrived:
            do_copy.wait()
            arrived.append(True)
        gh = jnp.concatenate([do_s[rows, c] for c in head_cols], 0)
        gh = (gh.astype(f32) * inv).astype(bf16)
        g_s[u] = gh
        delta = jnp.sum(gh.astype(f32) * ob.astype(f32), 1, keepdims=True)
        yield
        grad = None
        for i, (a, b) in enumerate(chunks):
            x = dot(g_s[u], va[g, a:b], NT)
            ds = (kept[i] * (x - delta)).astype(bf16)
            ds_s[u, :, a:b] = ds
            t = dot(ds, ka[g, a:b], NN)
            grad = t if grad is None else grad + t
            yield
        grad = (grad * SCALE).astype(bf16)
        for c, s in zip(head_cols, head_rows):
            dq_ref[0, rows, c] = grad[s]
        for a, b in chunks:
            dv = dot(p_s[u, :, a:b], g_s[u], TN)
            dk = dot(ds_s[u, :, a:b], q_s[u], TN)
            if half == 0:
                dv_s[g, a:b], dk_s[g, a:b] = dv, dk
            else:
                e, f = min(b, first), max(a, first)
                if e > a:
                    dv_s[g, a:e] += dv[: e - a]
                    dk_s[g, a:e] += dk[: e - a]
                if b > f:
                    dv_s[g, f:b], dk_s[g, f:b] = dv[f - a :], dk[f - a :]
            yield

    chains = [chain(g, half) for g in range(kv_heads) for half in range(2)]
    live = list(range(len(chains)))
    step = 0
    while live:
        for i in list(live):
            if step >= i * LEAD and next(chains[i], chains) is chains:
                live.remove(i)
        step += 1
    pieces = (cores, block_rows, D)
    for g in range(kv_heads):
        cols = slice(g * D, (g + 1) * D)
        dk, dv = dk_s[g] * SCALE, dv_s[g]
        for k in range(parts):
            rows = slice(k * part_rows, (k + 1) * part_rows)
            dp_refs[k][:, :block_rows, cols] = dk[rows].astype(bf16).reshape(pieces)
            dp_refs[k][:, block_rows:, cols] = dv[rows].astype(bf16).reshape(pieces)
        dkr_ref[0, :, cols] = dk[prompt_len:].astype(bf16)
        dvr_ref[0, :, cols] = dv[prompt_len:].astype(bf16)


def attend(slot, lengths, queries, out_grad, resp_keys, resp_values, prompt_parts, done):
    D = HEAD_SIZE
    _, token_rows, width = queries.shape
    kv_width = resp_keys.shape[2]
    kv_heads = kv_width // D
    parts = len(prompt_parts)
    cores, both_rows, _ = prompt_parts[0].shape
    keys = parts * cores * both_rows // 2 + token_rows
    stack = width // kv_width * HALF

    def block(w):
        return pl.BlockSpec((1, token_rows, w), lambda i: (slot, 0, 0))

    sds = jax.ShapeDtypeStruct
    like = (queries, queries, resp_keys, resp_keys)
    outs = pl.pallas_call(
        functools.partial(attn_kernel, slot, parts),
        grid=(1,),
        in_specs=[SCALARS, WHOLE, HBM, WHOLE, WHOLE] + [WHOLE] * parts + [ANY] * len(done),
        out_specs=[block(x.shape[2]) for x in like] + [WHOLE] * parts,
        out_shape=[sds(x.shape, bf16) for x in like] + [sds(prompt_parts[0].shape, bf16)] * parts,
        input_output_aliases={5 + parts + i: i for i in range(len(done))},
        scratch_shapes=[
            pltpu.VMEM((2 * kv_heads, stack, keys), bf16),
            pltpu.VMEM((2 * kv_heads, stack, keys), bf16),
            pltpu.VMEM((2 * kv_heads, stack, D), bf16),
            pltpu.VMEM((2 * kv_heads, stack, D), bf16),
            pltpu.VMEM((kv_heads, keys, D), bf16),
            pltpu.VMEM((kv_heads, keys, D), bf16),
            pltpu.VMEM((kv_heads, keys, D), f32),
            pltpu.VMEM((kv_heads, keys, D), f32),
            pltpu.VMEM((token_rows, width), bf16),
            pltpu.SemaphoreType.DMA,
        ],
        compiler_params=pltpu.CompilerParams(
            vmem_limit_bytes=ATTN_VMEM, dimension_semantics=("arbitrary",)
        ),
        cost_estimate=pl.CostEstimate(
            flops=12 * token_rows * keys * width, bytes_accessed=8 * token_rows * width, transcendentals=0
        ),
        name="attn",
    )(lengths, queries, out_grad, resp_keys, resp_values, *prompt_parts, *done)
    return outs[:4], outs[4:]


def local(
    planes,
    queries,
    resp_keys,
    response_values,
    prompt_key_rows,
    prompt_value_rows,
    out_grad,
    group_list,
    lengths,
):
    dp = lax.axis_size("dp")
    per_plane = dp // planes
    chips = per_plane // 2
    count = queries.shape[0]
    me = lax.axis_index("dp")
    plane, chip, core = me // per_plane, me % per_plane // 2, me % 2

    def shift(v, k):
        return lax.ppermute(v, "dp", [(i, (i + k * per_plane) % dp) for i in range(dp)])

    def turn(v, k):
        pairs = [
            (i, i // per_plane * per_plane + (i % per_plane + 2 * k) % per_plane) for i in range(dp)
        ]
        return lax.ppermute(v, "dp", pairs)

    def swap(v):
        return lax.ppermute(v, "dp", [(i, i ^ 1) for i in range(dp)])

    there = (chip + jnp.arange(chips, dtype=jnp.int32)) % chips
    cores = jnp.stack([core, 1 - core])
    device = (plane * chips + there[None, :]) * 2 + cores[:, None]
    ids = (device[:, :, None] * count + jnp.arange(count, dtype=jnp.int32)).reshape(-1)
    member = group_list[:, :, None] == ids[None, None, :]
    above = (jnp.arange(planes, dtype=jnp.int32) - plane) % planes

    def by_prompt(value):
        return jnp.sum(jnp.where(member, value[:, None, None], 0), axis=(0, 1))

    key_rows, kv_width = prompt_key_rows.shape
    rows = 2 * key_rows
    zero = jnp.zeros((), bf16)
    mine = lax.pad(prompt_key_rows, zero, ((0, key_rows, 0), (0, 0, 0))) + lax.pad(
        prompt_value_rows, zero, ((key_rows, 0, 0), (0, 0, 0))
    )
    half_turn = shift(mine, 4)
    from2, from6 = shift(mine, -2), shift(mine, 2)
    both = jnp.concatenate([mine, half_turn], 0)
    from1, from7 = shift(both, -1), shift(both, 1)
    order = [0, 4, 1, 5, 7, 3, 2, 6]
    place = sum(jnp.where(above == d, at, 0) for at, d in enumerate(order))
    pieces = jnp.concatenate([both, from1, from7, from2, from6], 0).reshape(planes, rows, kv_width)
    partner = swap(pieces)
    sends = chips * count
    picked = pl.pallas_call(
        pick_kernel,
        in_specs=[SCALARS, WHOLE, WHOLE],
        out_specs=[WHOLE] * sends,
        out_shape=[jax.ShapeDtypeStruct((2, rows, kv_width), bf16)] * sends,
        compiler_params=pltpu.CompilerParams(vmem_limit_bytes=4 * 2**20),
        name="pick",
    )(by_prompt(place), pieces, partner)
    prompts = [
        [picked[r]] + [turn(picked[k * count + r], k) for k in range(1, chips)]
        for r in range(count)
    ]

    written, back = [], []
    for r in range(count):
        written, grads = attend(
            r, lengths, queries, out_grad, resp_keys, response_values, prompts[r], written
        )
        if back:
            grads, back[-1] = lax.optimization_barrier((grads, back[-1]))
        back.append([grads[0]] + [turn(grads[k], -k) for k in range(1, chips)])
    terms = [jnp.stack([g[0] for g in parts]) for parts in back]
    partner_terms = [swap(jnp.stack([g[1] for g in parts])) for parts in back]
    attn_out, grad_q, grad_k, grad_v = written

    by_slot = by_prompt(above).reshape(2, chips, count).transpose(0, 2, 1).reshape(-1)
    sds = jax.ShapeDtypeStruct
    up, down, up2, down2, keep = pl.pallas_call(
        fold_kernel,
        in_specs=[SCALARS] + [WHOLE] * (2 * count),
        out_specs=[WHOLE] * 5,
        out_shape=[
            sds((2, rows, kv_width), bf16),
            sds((2, rows, kv_width), bf16),
            sds((rows, kv_width), bf16),
            sds((rows, kv_width), bf16),
            sds((2, rows, kv_width), f32),
        ],
        scratch_shapes=[pltpu.VMEM((planes, rows, kv_width), f32)],
        compiler_params=pltpu.CompilerParams(vmem_limit_bytes=8 * 2**20),
        name="fold",
    )(by_slot, *terms, *partner_terms)
    up, down = shift(up, 1), shift(down, -1)
    up2, down2 = shift(up2, 2), shift(down2, -2)
    far = shift((keep[1] + up[1].astype(f32) + down[1].astype(f32)).astype(bf16), 4)
    near = keep[0] + up[0].astype(f32) + down[0].astype(f32)
    total = near + up2.astype(f32) + down2.astype(f32) + far.astype(f32)
    total = total.astype(bf16)
    return attn_out, grad_q, grad_k, grad_v, total[:key_rows], total[key_rows:]


def solution(mesh):
    in_specs = (
        P("dp", None, "tensor"),
        P("dp", None, "tensor"),
        P("dp", None, "tensor"),
        P("dp", "tensor"),
        P("dp", "tensor"),
        P("dp", None, "tensor"),
        P(),
        P("dp"),
    )
    out_specs = (
        P("dp", None, "tensor"),
        P("dp", None, "tensor"),
        P("dp", None, "tensor"),
        P("dp", None, "tensor"),
        P("dp", "tensor"),
        P("dp", "tensor"),
    )

    def step(*args):
        planes = args[6].shape[0]
        return jax.shard_map(
            functools.partial(local, planes),
            mesh=mesh,
            in_specs=in_specs,
            out_specs=out_specs,
            check_vma=False,
        )(*args)

    return step
```

```python
import functools
import math

import jax
import jax.numpy as jnp
from jax import lax
from jax.experimental import pallas as pl
from jax.experimental.pallas import tpu as pltpu
from jax.sharding import PartitionSpec as P

HEAD_SIZE = 128
SCALE = HEAD_SIZE**-0.5
SCALE_LOG2 = SCALE * math.log2(math.e)
HALF = 128
CHUNK = 256
LEAD = 3
ATTN_VMEM = 28 * 2**20
NT = (((1,), (1,)), ((), ()))
NN = (((1,), (0,)), ((), ()))
TN = (((0,), (0,)), ((), ()))
f32 = jnp.float32
bf16 = jnp.bfloat16
WHOLE = pl.BlockSpec(memory_space=pltpu.VMEM)
ANY = pl.BlockSpec(memory_space=pl.ANY)
HBM = pl.BlockSpec(memory_space=pltpu.HBM)
SCALARS = pl.BlockSpec(memory_space=pltpu.SMEM)


def dot(a, b, dims):
    return lax.dot_general(a, b, dims, preferred_element_type=f32)


def pick_kernel(idx_ref, own_ref, partner_ref, *outs):
    for i, out in enumerate(outs):
        block = idx_ref[i]
        out[0] = own_ref[block]
        out[1] = partner_ref[block]


def fold_kernel(idx_ref, *refs):
    *terms, up_ref, down_ref, far_ref, keep_ref, total = refs
    total[...] = jnp.zeros_like(total)
    at = 0
    for term in terms:
        for k in range(term.shape[0]):
            d = idx_ref[at]
            total[d] = total[d] + term[k].astype(f32)
            at += 1
    up_ref[0], up_ref[1] = total[1].astype(bf16), total[3].astype(bf16)
    down_ref[0], down_ref[1] = total[7].astype(bf16), total[5].astype(bf16)
    far_ref[...] = total[4].astype(bf16)
    keep_ref[0], keep_ref[1], keep_ref[2] = total[0], total[2], total[6]


def attn_kernel(slot, parts, len_ref, q_ref, do_ref, kr_ref, vr_ref, *refs):
    part_refs, refs = refs[:parts], refs[parts:]
    refs = refs[0 if slot == 0 else 4 :]
    o_ref, dq_ref, dkr_ref, dvr_ref, *refs = refs
    dp_refs, refs = refs[:parts], refs[parts:]
    p_s, ds_s, g_s, q_s, ka, va, dk_s, dv_s, do_s, do_sem, o_s, dq_s, out_sems = refs
    do_copy = pltpu.make_async_copy(do_ref.at[slot], do_s, do_sem)
    do_copy.start()
    arrived, leaving = [], []
    D = HEAD_SIZE
    kv_heads = kr_ref.shape[2] // D
    heads = q_ref.shape[2] // (D * kv_heads)
    cores, both_rows, _ = part_refs[0].shape
    block_rows = both_rows // 2
    part_rows = cores * block_rows
    prompt_len = parts * part_rows
    n = len_ref[slot]
    for g in range(kv_heads):
        cols = slice(g * D, (g + 1) * D)
        for k in range(parts):
            rows = slice(k * part_rows, (k + 1) * part_rows)
            ka[g, rows] = part_refs[k][:, :block_rows, cols].reshape(part_rows, D)
            va[g, rows] = part_refs[k][:, block_rows:, cols].reshape(part_rows, D)
        ka[g, prompt_len:] = kr_ref[slot, :, cols]
        va[g, prompt_len:] = vr_ref[slot, :, cols]
    row = lax.broadcasted_iota(jnp.int32, (HALF, HALF), 0)
    col = lax.broadcasted_iota(jnp.int32, (HALF, HALF), 1)
    tri = jnp.concatenate([col <= row] * heads, 0)
    rid = lax.broadcasted_iota(jnp.int32, (HALF, 1), 0)
    first = prompt_len + HALF

    def leave(held, out_ref, rows, g):
        cols = slice(g * heads * D, (g + 1) * heads * D)
        copy = pltpu.make_async_copy(
            held.at[rows, cols], out_ref.at[slot, rows, cols], out_sems.at[len(leaving)]
        )
        copy.start()
        leaving.append(copy)

    def chain(g, half):
        u = 2 * g + half
        j = first + HALF * half
        rows = slice(half * HALF, (half + 1) * HALF)
        head_cols = [slice((g * heads + h) * D, (g * heads + h + 1) * D) for h in range(heads)]
        head_rows = [slice(h * HALF, (h + 1) * HALF) for h in range(heads)]
        q_s[u] = jnp.concatenate([q_ref[slot, rows, c] for c in head_cols], 0)
        chunks = [(a, min(a + CHUNK, j)) for a in range(0, j, CHUNK)]
        top, kept = None, []
        for a, b in chunks:
            s = dot(q_s[u], ka[g, a:b], NT)
            if b == j:
                last = jnp.where(tri, s[:, b - a - HALF :], -jnp.inf)
                s = jnp.concatenate([s[:, : b - a - HALF], last], 1) if b - a > HALF else last
            kept.append(s)
            for k in range(0, b - a, HALF):
                part = s[:, k : k + HALF]
                top = part if top is None else jnp.maximum(top, part)
            yield
        m = jnp.max(top, 1, keepdims=True) * SCALE_LOG2
        yield
        norm, out = None, None
        for i, (a, b) in enumerate(chunks):
            p = jnp.exp2(kept[i] * SCALE_LOG2 - m)
            kept[i] = p
            for k in range(0, b - a, HALF):
                part = p[:, k : k + HALF]
                norm = part if norm is None else norm + part
            pb = p.astype(bf16)
            p_s[u, :, a:b] = pb
            t = dot(pb, va[g, a:b], NN)
            out = t if out is None else out + t
            yield
        valid = jnp.concatenate([(rid + half * HALF < n).astype(f32)] * heads, 0)
        inv = valid / jnp.sum(norm, 1, keepdims=True)
        ob = (out * inv).astype(bf16)
        for c, s in zip(head_cols, head_rows):
            o_s[rows, c] = ob[s]
        leave(o_s, o_ref, rows, g)
        if not arrived:
            do_copy.wait()
            arrived.append(True)
        gh = jnp.concatenate([do_s[rows, c] for c in head_cols], 0)
        gh = (gh.astype(f32) * inv).astype(bf16)
        g_s[u] = gh
        delta = jnp.sum(gh.astype(f32) * ob.astype(f32), 1, keepdims=True)
        yield
        grad = None
        for i, (a, b) in enumerate(chunks):
            x = dot(g_s[u], va[g, a:b], NT)
            ds = (kept[i] * (x - delta)).astype(bf16)
            ds_s[u, :, a:b] = ds
            t = dot(ds, ka[g, a:b], NN)
            grad = t if grad is None else grad + t
            yield
        grad = (grad * SCALE).astype(bf16)
        for c, s in zip(head_cols, head_rows):
            dq_s[rows, c] = grad[s]
        leave(dq_s, dq_ref, rows, g)
        for a, b in chunks:
            dv = dot(p_s[u, :, a:b], g_s[u], TN)
            dk = dot(ds_s[u, :, a:b], q_s[u], TN)
            if half == 0:
                dv_s[g, a:b], dk_s[g, a:b] = dv, dk
            else:
                e, f = min(b, first), max(a, first)
                if e > a:
                    dv_s[g, a:e] += dv[: e - a]
                    dk_s[g, a:e] += dk[: e - a]
                if b > f:
                    dv_s[g, f:b], dk_s[g, f:b] = dv[f - a :], dk[f - a :]
            yield

    chains = [chain(g, half) for g in range(kv_heads) for half in range(2)]
    live = list(range(len(chains)))
    step = 0
    while live:
        for i in list(live):
            if step >= i * LEAD and next(chains[i], chains) is chains:
                live.remove(i)
        step += 1
    pieces = (cores, block_rows, D)
    for g in range(kv_heads):
        cols = slice(g * D, (g + 1) * D)
        dk, dv = dk_s[g] * SCALE, dv_s[g]
        for k in range(parts):
            rows = slice(k * part_rows, (k + 1) * part_rows)
            dp_refs[k][:, :block_rows, cols] = dk[rows].astype(bf16).reshape(pieces)
            dp_refs[k][:, block_rows:, cols] = dv[rows].astype(bf16).reshape(pieces)
        dkr_ref[0, :, cols] = dk[prompt_len:].astype(bf16)
        dvr_ref[0, :, cols] = dv[prompt_len:].astype(bf16)
    for copy in leaving:
        copy.wait()


def attend(slot, lengths, queries, out_grad, resp_keys, resp_values, prompt_parts, done):
    D = HEAD_SIZE
    _, token_rows, width = queries.shape
    kv_width = resp_keys.shape[2]
    kv_heads = kv_width // D
    parts = len(prompt_parts)
    cores, both_rows, _ = prompt_parts[0].shape
    keys = parts * cores * both_rows // 2 + token_rows
    stack = width // kv_width * HALF

    def block(w):
        return pl.BlockSpec((1, token_rows, w), lambda i: (slot, 0, 0))

    sds = jax.ShapeDtypeStruct
    like = (queries, queries, resp_keys, resp_keys)
    outs = pl.pallas_call(
        functools.partial(attn_kernel, slot, parts),
        grid=(1,),
        in_specs=[SCALARS, WHOLE, HBM, WHOLE, WHOLE] + [WHOLE] * parts + [ANY] * len(done),
        out_specs=[HBM, HBM, block(kv_width), block(kv_width)] + [WHOLE] * parts,
        out_shape=[sds(x.shape, bf16) for x in like] + [sds(prompt_parts[0].shape, bf16)] * parts,
        input_output_aliases={5 + parts + i: i for i in range(len(done))},
        scratch_shapes=[
            pltpu.VMEM((2 * kv_heads, stack, keys), bf16),
            pltpu.VMEM((2 * kv_heads, stack, keys), bf16),
            pltpu.VMEM((2 * kv_heads, stack, D), bf16),
            pltpu.VMEM((2 * kv_heads, stack, D), bf16),
            pltpu.VMEM((kv_heads, keys, D), bf16),
            pltpu.VMEM((kv_heads, keys, D), bf16),
            pltpu.VMEM((kv_heads, keys, D), f32),
            pltpu.VMEM((kv_heads, keys, D), f32),
            pltpu.VMEM((token_rows, width), bf16),
            pltpu.SemaphoreType.DMA,
            pltpu.VMEM((token_rows, width), bf16),
            pltpu.VMEM((token_rows, width), bf16),
            pltpu.SemaphoreType.DMA((4 * kv_heads,)),
        ],
        compiler_params=pltpu.CompilerParams(
            vmem_limit_bytes=ATTN_VMEM, dimension_semantics=("arbitrary",)
        ),
        cost_estimate=pl.CostEstimate(
            flops=12 * token_rows * keys * width, bytes_accessed=8 * token_rows * width, transcendentals=0
        ),
        name="attn",
    )(lengths, queries, out_grad, resp_keys, resp_values, *prompt_parts, *done)
    return outs[:4], outs[4:]


def local(
    planes,
    queries,
    resp_keys,
    response_values,
    prompt_key_rows,
    prompt_value_rows,
    out_grad,
    group_list,
    lengths,
):
    dp = lax.axis_size("dp")
    per_plane = dp // planes
    chips = per_plane // 2
    count = queries.shape[0]
    me = lax.axis_index("dp")
    plane, chip, core = me // per_plane, me % per_plane // 2, me % 2

    def shift(v, k):
        return lax.ppermute(v, "dp", [(i, (i + k * per_plane) % dp) for i in range(dp)])

    def turn(v, k):
        pairs = [
            (i, i // per_plane * per_plane + (i % per_plane + 2 * k) % per_plane) for i in range(dp)
        ]
        return lax.ppermute(v, "dp", pairs)

    def swap(v):
        return lax.ppermute(v, "dp", [(i, i ^ 1) for i in range(dp)])

    there = (chip + jnp.arange(chips, dtype=jnp.int32)) % chips
    cores = jnp.stack([core, 1 - core])
    device = (plane * chips + there[None, :]) * 2 + cores[:, None]
    ids = (device[:, :, None] * count + jnp.arange(count, dtype=jnp.int32)).reshape(-1)
    member = group_list[:, :, None] == ids[None, None, :]
    above = (jnp.arange(planes, dtype=jnp.int32) - plane) % planes

    def by_prompt(value):
        return jnp.sum(jnp.where(member, value[:, None, None], 0), axis=(0, 1))

    key_rows, kv_width = prompt_key_rows.shape
    rows = 2 * key_rows
    zero = jnp.zeros((), bf16)
    mine = lax.pad(prompt_key_rows, zero, ((0, key_rows, 0), (0, 0, 0))) + lax.pad(
        prompt_value_rows, zero, ((key_rows, 0, 0), (0, 0, 0))
    )
    from2, from6 = shift(mine, -2), shift(mine, 2)
    from4 = shift(mine, 4)
    from1 = shift(jnp.concatenate([mine, from2], 0), -1)
    from7 = shift(jnp.concatenate([mine, from6], 0), 1)
    order = [0, 2, 6, 1, 3, 7, 5, 4]
    place = sum(jnp.where(above == d, at, 0) for at, d in enumerate(order))
    pieces = jnp.concatenate([mine, from2, from6, from1, from7, from4], 0).reshape(planes, rows, kv_width)
    partner = swap(pieces)
    sends = chips * count
    picked = pl.pallas_call(
        pick_kernel,
        in_specs=[SCALARS, WHOLE, WHOLE],
        out_specs=[WHOLE] * sends,
        out_shape=[jax.ShapeDtypeStruct((2, rows, kv_width), bf16)] * sends,
        compiler_params=pltpu.CompilerParams(vmem_limit_bytes=4 * 2**20),
        name="pick",
    )(by_prompt(place), pieces, partner)
    prompts = [
        [picked[r]] + [turn(picked[k * count + r], k) for k in range(1, chips)]
        for r in range(count)
    ]

    out_grad = pltpu.with_memory_space_constraint(out_grad, pltpu.HBM)
    written, back = [], []
    for r in range(count):
        written, grads = attend(
            r, lengths, queries, out_grad, resp_keys, response_values, prompts[r], written
        )
        if back:
            grads, back[-1] = lax.optimization_barrier((grads, back[-1]))
        back.append([grads[0]] + [turn(grads[k], -k) for k in range(1, chips)])
    terms = [jnp.stack([g[0] for g in parts]) for parts in back]
    partner_terms = [swap(jnp.stack([g[1] for g in parts])) for parts in back]
    attn_out, grad_q, grad_k, grad_v = written

    by_slot = by_prompt(above).reshape(2, chips, count).transpose(0, 2, 1).reshape(-1)
    sds = jax.ShapeDtypeStruct
    up, down, far, keep = pl.pallas_call(
        fold_kernel,
        in_specs=[SCALARS] + [WHOLE] * (2 * count),
        out_specs=[WHOLE] * 4,
        out_shape=[
            sds((2, rows, kv_width), bf16),
            sds((2, rows, kv_width), bf16),
            sds((rows, kv_width), bf16),
            sds((3, rows, kv_width), f32),
        ],
        scratch_shapes=[pltpu.VMEM((planes, rows, kv_width), f32)],
        compiler_params=pltpu.CompilerParams(vmem_limit_bytes=8 * 2**20),
        name="fold",
    )(by_slot, *terms, *partner_terms)
    up, down = shift(up, 1), shift(down, -1)
    far = shift(far, 4)
    up2 = shift((keep[1] + up[1].astype(f32)).astype(bf16), 2)
    down2 = shift((keep[2] + down[1].astype(f32)).astype(bf16), -2)
    near = keep[0] + up[0].astype(f32) + down[0].astype(f32)
    total = near + up2.astype(f32) + down2.astype(f32) + far.astype(f32)
    total = total.astype(bf16)
    return attn_out, grad_q, grad_k, grad_v, total[:key_rows], total[key_rows:]


def solution(mesh):
    in_specs = (
        P("dp", None, "tensor"),
        P("dp", None, "tensor"),
        P("dp", None, "tensor"),
        P("dp", "tensor"),
        P("dp", "tensor"),
        P("dp", None, "tensor"),
        P(),
        P("dp"),
    )
    out_specs = (
        P("dp", None, "tensor"),
        P("dp", None, "tensor"),
        P("dp", None, "tensor"),
        P("dp", None, "tensor"),
        P("dp", "tensor"),
        P("dp", "tensor"),
    )

    def step(*args):
        planes = args[6].shape[0]
        return jax.shard_map(
            functools.partial(local, planes),
            mesh=mesh,
            in_specs=in_specs,
            out_specs=out_specs,
            check_vma=False,
        )(*args)

    return step
```

```python
import functools
import math

import jax
import jax.numpy as jnp
from jax import lax
from jax.experimental import pallas as pl
from jax.experimental.pallas import tpu as pltpu
from jax.sharding import PartitionSpec as P

HEAD_SIZE = 128
SCALE = HEAD_SIZE**-0.5
SCALE_LOG2 = SCALE * math.log2(math.e)
HALF = 128
CHUNK = 256
LEAD = 3
ATTN_VMEM = 28 * 2**20
NT = (((1,), (1,)), ((), ()))
NN = (((1,), (0,)), ((), ()))
TN = (((0,), (0,)), ((), ()))
f32 = jnp.float32
bf16 = jnp.bfloat16
WHOLE = pl.BlockSpec(memory_space=pltpu.VMEM)
ANY = pl.BlockSpec(memory_space=pl.ANY)
HBM = pl.BlockSpec(memory_space=pltpu.HBM)
SCALARS = pl.BlockSpec(memory_space=pltpu.SMEM)


def dot(a, b, dims):
    return lax.dot_general(a, b, dims, preferred_element_type=f32)


def pick_kernel(idx_ref, own_ref, partner_ref, *outs):
    for i, out in enumerate(outs):
        block = idx_ref[i]
        out[0] = own_ref[block]
        out[1] = partner_ref[block]


def fold_kernel(idx_ref, *refs):
    *terms, up_ref, down_ref, far_ref, keep_ref, total = refs
    total[...] = jnp.zeros_like(total)
    at = 0
    for term in terms:
        for k in range(term.shape[0]):
            d = idx_ref[at]
            total[d] = total[d] + term[k].astype(f32)
            at += 1
    up_ref[0], up_ref[1] = total[1].astype(bf16), total[3].astype(bf16)
    down_ref[0], down_ref[1] = total[7].astype(bf16), total[5].astype(bf16)
    far_ref[...] = total[4].astype(bf16)
    keep_ref[0], keep_ref[1], keep_ref[2] = total[0], total[2], total[6]


def attn_kernel(slot, parts, len_ref, q_ref, do_ref, kr_ref, vr_ref, *refs):
    part_refs, refs = refs[:parts], refs[parts:]
    refs = refs[0 if slot == 0 else 4 :]
    o_ref, dq_ref, dkr_ref, dvr_ref, *refs = refs
    dp_refs, refs = refs[:parts], refs[parts:]
    p_s, ds_s, g_s, q_s, ka, va, dk_s, dv_s = refs
    D = HEAD_SIZE
    kv_heads = kr_ref.shape[2] // D
    heads = q_ref.shape[2] // (D * kv_heads)
    cores, both_rows, _ = part_refs[0].shape
    block_rows = both_rows // 2
    part_rows = cores * block_rows
    prompt_len = parts * part_rows
    n = len_ref[slot]
    for g in range(kv_heads):
        cols = slice(g * D, (g + 1) * D)
        for k in range(parts):
            rows = slice(k * part_rows, (k + 1) * part_rows)
            ka[g, rows] = part_refs[k][:, :block_rows, cols].reshape(part_rows, D)
            va[g, rows] = part_refs[k][:, block_rows:, cols].reshape(part_rows, D)
        ka[g, prompt_len:] = kr_ref[slot, :, cols]
        va[g, prompt_len:] = vr_ref[slot, :, cols]
    row = lax.broadcasted_iota(jnp.int32, (HALF, HALF), 0)
    col = lax.broadcasted_iota(jnp.int32, (HALF, HALF), 1)
    tri = jnp.concatenate([col <= row] * heads, 0)
    rid = lax.broadcasted_iota(jnp.int32, (HALF, 1), 0)
    first = prompt_len + HALF

    def chain(g, half):
        u = 2 * g + half
        j = first + HALF * half
        rows = slice(half * HALF, (half + 1) * HALF)
        head_cols = [slice((g * heads + h) * D, (g * heads + h + 1) * D) for h in range(heads)]
        head_rows = [slice(h * HALF, (h + 1) * HALF) for h in range(heads)]
        q_s[u] = jnp.concatenate([q_ref[slot, rows, c] for c in head_cols], 0)
        chunks = [(a, min(a + CHUNK, j)) for a in range(0, j, CHUNK)]
        top, kept = None, []
        for a, b in chunks:
            s = dot(q_s[u], ka[g, a:b], NT)
            if b == j:
                last = jnp.where(tri, s[:, b - a - HALF :], -jnp.inf)
                s = jnp.concatenate([s[:, : b - a - HALF], last], 1) if b - a > HALF else last
            kept.append(s)
            for k in range(0, b - a, HALF):
                part = s[:, k : k + HALF]
                top = part if top is None else jnp.maximum(top, part)
            yield
        m = jnp.max(top, 1, keepdims=True) * SCALE_LOG2
        yield
        norm, out = None, None
        for i, (a, b) in enumerate(chunks):
            p = jnp.exp2(kept[i] * SCALE_LOG2 - m)
            kept[i] = p
            for k in range(0, b - a, HALF):
                part = p[:, k : k + HALF]
                norm = part if norm is None else norm + part
            pb = p.astype(bf16)
            p_s[u, :, a:b] = pb
            t = dot(pb, va[g, a:b], NN)
            out = t if out is None else out + t
            yield
        valid = jnp.concatenate([(rid + half * HALF < n).astype(f32)] * heads, 0)
        inv = valid / jnp.sum(norm, 1, keepdims=True)
        ob = (out * inv).astype(bf16)
        for c, s in zip(head_cols, head_rows):
            o_ref[0, rows, c] = ob[s]
        gh = jnp.concatenate([do_ref[0, rows, c] for c in head_cols], 0)
        gh = (gh.astype(f32) * inv).astype(bf16)
        g_s[u] = gh
        delta = jnp.sum(gh.astype(f32) * ob.astype(f32), 1, keepdims=True)
        yield
        grad = None
        for i, (a, b) in enumerate(chunks):
            x = dot(g_s[u], va[g, a:b], NT)
            ds = (kept[i] * (x - delta)).astype(bf16)
            ds_s[u, :, a:b] = ds
            t = dot(ds, ka[g, a:b], NN)
            grad = t if grad is None else grad + t
            yield
        grad = (grad * SCALE).astype(bf16)
        for c, s in zip(head_cols, head_rows):
            dq_ref[0, rows, c] = grad[s]
        for a, b in chunks:
            dv = dot(p_s[u, :, a:b], g_s[u], TN)
            dk = dot(ds_s[u, :, a:b], q_s[u], TN)
            if half == 0:
                dv_s[g, a:b], dk_s[g, a:b] = dv, dk
            else:
                e, f = min(b, first), max(a, first)
                if e > a:
                    dv_s[g, a:e] += dv[: e - a]
                    dk_s[g, a:e] += dk[: e - a]
                if b > f:
                    dv_s[g, f:b], dk_s[g, f:b] = dv[f - a :], dk[f - a :]
            yield

    chains = [chain(g, half) for g in range(kv_heads) for half in range(2)]
    live = list(range(len(chains)))
    step = 0
    while live:
        for i in list(live):
            if step >= i * LEAD and next(chains[i], chains) is chains:
                live.remove(i)
        step += 1
    pieces = (cores, block_rows, D)
    for g in range(kv_heads):
        cols = slice(g * D, (g + 1) * D)
        dk, dv = dk_s[g] * SCALE, dv_s[g]
        for k in range(parts):
            rows = slice(k * part_rows, (k + 1) * part_rows)
            dp_refs[k][:, :block_rows, cols] = dk[rows].astype(bf16).reshape(pieces)
            dp_refs[k][:, block_rows:, cols] = dv[rows].astype(bf16).reshape(pieces)
        dkr_ref[0, :, cols] = dk[prompt_len:].astype(bf16)
        dvr_ref[0, :, cols] = dv[prompt_len:].astype(bf16)


def attend(slot, lengths, queries, out_grad, resp_keys, resp_values, prompt_parts, done):
    D = HEAD_SIZE
    _, token_rows, width = queries.shape
    kv_width = resp_keys.shape[2]
    kv_heads = kv_width // D
    parts = len(prompt_parts)
    cores, both_rows, _ = prompt_parts[0].shape
    keys = parts * cores * both_rows // 2 + token_rows
    stack = width // kv_width * HALF

    def block(w):
        return pl.BlockSpec((1, token_rows, w), lambda i: (slot, 0, 0))

    sds = jax.ShapeDtypeStruct
    like = (queries, queries, resp_keys, resp_keys)
    outs = pl.pallas_call(
        functools.partial(attn_kernel, slot, parts),
        grid=(1,),
        in_specs=[SCALARS, WHOLE, block(width), WHOLE, WHOLE] + [WHOLE] * parts + [ANY] * len(done),
        out_specs=[block(x.shape[2]) for x in like] + [WHOLE] * parts,
        out_shape=[sds(x.shape, bf16) for x in like] + [sds(prompt_parts[0].shape, bf16)] * parts,
        input_output_aliases={5 + parts + i: i for i in range(len(done))},
        scratch_shapes=[
            pltpu.VMEM((2 * kv_heads, stack, keys), bf16),
            pltpu.VMEM((2 * kv_heads, stack, keys), bf16),
            pltpu.VMEM((2 * kv_heads, stack, D), bf16),
            pltpu.VMEM((2 * kv_heads, stack, D), bf16),
            pltpu.VMEM((kv_heads, keys, D), bf16),
            pltpu.VMEM((kv_heads, keys, D), bf16),
            pltpu.VMEM((kv_heads, keys, D), f32),
            pltpu.VMEM((kv_heads, keys, D), f32),
        ],
        compiler_params=pltpu.CompilerParams(
            vmem_limit_bytes=ATTN_VMEM, dimension_semantics=("arbitrary",)
        ),
        cost_estimate=pl.CostEstimate(
            flops=12 * token_rows * keys * width, bytes_accessed=8 * token_rows * width, transcendentals=0
        ),
        name="attn",
    )(lengths, queries, out_grad, resp_keys, resp_values, *prompt_parts, *done)
    return outs[:4], outs[4:]


def local(
    planes,
    queries,
    resp_keys,
    response_values,
    prompt_key_rows,
    prompt_value_rows,
    out_grad,
    group_list,
    lengths,
):
    dp = lax.axis_size("dp")
    per_plane = dp // planes
    chips = per_plane // 2
    count = queries.shape[0]
    me = lax.axis_index("dp")
    plane, chip, core = me // per_plane, me % per_plane // 2, me % 2

    def shift(v, k):
        return lax.ppermute(v, "dp", [(i, (i + k * per_plane) % dp) for i in range(dp)])

    def turn(v, k):
        pairs = [
            (i, i // per_plane * per_plane + (i % per_plane + 2 * k) % per_plane) for i in range(dp)
        ]
        return lax.ppermute(v, "dp", pairs)

    def swap(v):
        return lax.ppermute(v, "dp", [(i, i ^ 1) for i in range(dp)])

    there = (chip + jnp.arange(chips, dtype=jnp.int32)) % chips
    cores = jnp.stack([core, 1 - core])
    device = (plane * chips + there[None, :]) * 2 + cores[:, None]
    ids = (device[:, :, None] * count + jnp.arange(count, dtype=jnp.int32)).reshape(-1)
    member = group_list[:, :, None] == ids[None, None, :]
    above = (jnp.arange(planes, dtype=jnp.int32) - plane) % planes

    def by_prompt(value):
        return jnp.sum(jnp.where(member, value[:, None, None], 0), axis=(0, 1))

    key_rows, kv_width = prompt_key_rows.shape
    rows = 2 * key_rows
    zero = jnp.zeros((), bf16)
    mine = lax.pad(prompt_key_rows, zero, ((0, key_rows, 0), (0, 0, 0))) + lax.pad(
        prompt_value_rows, zero, ((key_rows, 0, 0), (0, 0, 0))
    )
    from2, from6 = shift(mine, -2), shift(mine, 2)
    late, from6 = lax.optimization_barrier((mine, from6))
    from4 = shift(late, 4)
    from1 = shift(jnp.concatenate([mine, from2], 0), -1)
    from7 = shift(jnp.concatenate([mine, from6], 0), 1)
    order = [0, 2, 6, 1, 3, 7, 5, 4]
    place = sum(jnp.where(above == d, at, 0) for at, d in enumerate(order))
    pieces = jnp.concatenate([mine, from2, from6, from1, from7, from4], 0).reshape(planes, rows, kv_width)
    partner = swap(pieces)
    sends = chips * count
    picked = pl.pallas_call(
        pick_kernel,
        in_specs=[SCALARS, WHOLE, WHOLE],
        out_specs=[WHOLE] * sends,
        out_shape=[jax.ShapeDtypeStruct((2, rows, kv_width), bf16)] * sends,
        compiler_params=pltpu.CompilerParams(vmem_limit_bytes=4 * 2**20),
        name="pick",
    )(by_prompt(place), pieces, partner)
    prompts = [
        [picked[r]] + [turn(picked[k * count + r], k) for k in range(1, chips)]
        for r in range(count)
    ]

    out_grad = pltpu.with_memory_space_constraint(out_grad, pltpu.HBM)
    written, back = [], []
    for r in range(count):
        written, grads = attend(
            r, lengths, queries, out_grad, resp_keys, response_values, prompts[r], written
        )
        if back:
            grads, back[-1] = lax.optimization_barrier((grads, back[-1]))
        back.append([grads[0]] + [turn(grads[k], -k) for k in range(1, chips)])
    terms = [jnp.stack([g[0] for g in parts]) for parts in back]
    partner_terms = [swap(jnp.stack([g[1] for g in parts])) for parts in back]
    attn_out, grad_q, grad_k, grad_v = written

    by_slot = by_prompt(above).reshape(2, chips, count).transpose(0, 2, 1).reshape(-1)
    sds = jax.ShapeDtypeStruct
    up, down, far, keep = pl.pallas_call(
        fold_kernel,
        in_specs=[SCALARS] + [WHOLE] * (2 * count),
        out_specs=[WHOLE] * 4,
        out_shape=[
            sds((2, rows, kv_width), bf16),
            sds((2, rows, kv_width), bf16),
            sds((rows, kv_width), bf16),
            sds((3, rows, kv_width), f32),
        ],
        scratch_shapes=[pltpu.VMEM((planes, rows, kv_width), f32)],
        compiler_params=pltpu.CompilerParams(vmem_limit_bytes=8 * 2**20),
        name="fold",
    )(by_slot, *terms, *partner_terms)
    up, down = shift(up, 1), shift(down, -1)
    far = shift(far, 4)
    up2 = shift((keep[1] + up[1].astype(f32)).astype(bf16), 2)
    down2 = shift((keep[2] + down[1].astype(f32)).astype(bf16), -2)
    near = keep[0] + up[0].astype(f32) + down[0].astype(f32)
    total = near + up2.astype(f32) + down2.astype(f32) + far.astype(f32)
    total = total.astype(bf16)
    return attn_out, grad_q, grad_k, grad_v, total[:key_rows], total[key_rows:]


def solution(mesh):
    in_specs = (
        P("dp", None, "tensor"),
        P("dp", None, "tensor"),
        P("dp", None, "tensor"),
        P("dp", "tensor"),
        P("dp", "tensor"),
        P("dp", None, "tensor"),
        P(),
        P("dp"),
    )
    out_specs = (
        P("dp", None, "tensor"),
        P("dp", None, "tensor"),
        P("dp", None, "tensor"),
        P("dp", None, "tensor"),
        P("dp", "tensor"),
        P("dp", "tensor"),
    )

    def step(*args):
        planes = args[6].shape[0]
        return jax.shard_map(
            functools.partial(local, planes),
            mesh=mesh,
            in_specs=in_specs,
            out_specs=out_specs,
            check_vma=False,
        )(*args)

    return step
```

```python
import functools
import math

import jax
import jax.numpy as jnp
from jax import lax
from jax.experimental import pallas as pl
from jax.experimental.pallas import tpu as pltpu
from jax.sharding import PartitionSpec as P

HEAD_SIZE = 128
SCALE = HEAD_SIZE**-0.5
SCALE_LOG2 = SCALE * math.log2(math.e)
HALF = 128
CHUNK = 256
LEAD = 3
ATTN_VMEM = 28 * 2**20
NT = (((1,), (1,)), ((), ()))
NN = (((1,), (0,)), ((), ()))
TN = (((0,), (0,)), ((), ()))
f32 = jnp.float32
bf16 = jnp.bfloat16
WHOLE = pl.BlockSpec(memory_space=pltpu.VMEM)
ANY = pl.BlockSpec(memory_space=pl.ANY)
HBM = pl.BlockSpec(memory_space=pltpu.HBM)
SCALARS = pl.BlockSpec(memory_space=pltpu.SMEM)


def dot(a, b, dims):
    return lax.dot_general(a, b, dims, preferred_element_type=f32)


def pick_kernel(idx_ref, own_ref, partner_ref, *outs):
    for i, out in enumerate(outs):
        block = idx_ref[i]
        out[0] = own_ref[block]
        out[1] = partner_ref[block]


def fold_kernel(idx_ref, *refs):
    *terms, up_ref, down_ref, far_ref, keep_ref, total = refs
    total[...] = jnp.zeros_like(total)
    at = 0
    for term in terms:
        for k in range(term.shape[0]):
            d = idx_ref[at]
            total[d] = total[d] + term[k].astype(f32)
            at += 1
    up_ref[0], up_ref[1] = total[1].astype(bf16), total[3].astype(bf16)
    down_ref[0], down_ref[1] = total[7].astype(bf16), total[5].astype(bf16)
    far_ref[...] = total[4].astype(bf16)
    keep_ref[0], keep_ref[1], keep_ref[2] = total[0], total[2], total[6]


def attn_kernel(slot, parts, len_ref, q_ref, do_ref, kr_ref, vr_ref, *refs):
    part_refs, refs = refs[:parts], refs[parts:]
    refs = refs[0 if slot == 0 else 4 :]
    o_ref, dq_ref, dkr_ref, dvr_ref, *refs = refs
    dp_refs, refs = refs[:parts], refs[parts:]
    p_s, ds_s, g_s, q_s, ka, va, dk_s, dv_s = refs
    D = HEAD_SIZE
    kv_heads = kr_ref.shape[2] // D
    heads = q_ref.shape[2] // (D * kv_heads)
    cores, both_rows, _ = part_refs[0].shape
    block_rows = both_rows // 2
    part_rows = cores * block_rows
    prompt_len = parts * part_rows
    n = len_ref[slot]
    for g in range(kv_heads):
        cols = slice(g * D, (g + 1) * D)
        for k in range(parts):
            rows = slice(k * part_rows, (k + 1) * part_rows)
            ka[g, rows] = part_refs[k][:, :block_rows, cols].reshape(part_rows, D)
            va[g, rows] = part_refs[k][:, block_rows:, cols].reshape(part_rows, D)
        ka[g, prompt_len:] = kr_ref[slot, :, cols]
        va[g, prompt_len:] = vr_ref[slot, :, cols]
    row = lax.broadcasted_iota(jnp.int32, (HALF, HALF), 0)
    col = lax.broadcasted_iota(jnp.int32, (HALF, HALF), 1)
    tri = jnp.concatenate([col <= row] * heads, 0)
    rid = lax.broadcasted_iota(jnp.int32, (HALF, 1), 0)
    first = prompt_len + HALF

    def chain(g, half):
        u = 2 * g + half
        j = first + HALF * half
        rows = slice(half * HALF, (half + 1) * HALF)
        head_cols = [slice((g * heads + h) * D, (g * heads + h + 1) * D) for h in range(heads)]
        head_rows = [slice(h * HALF, (h + 1) * HALF) for h in range(heads)]
        q_s[u] = jnp.concatenate([q_ref[slot, rows, c] for c in head_cols], 0)
        chunks = [(a, min(a + CHUNK, j)) for a in range(0, j, CHUNK)]
        top, kept = None, []
        for a, b in chunks:
            s = dot(q_s[u], ka[g, a:b], NT)
            if b == j:
                last = jnp.where(tri, s[:, b - a - HALF :], -jnp.inf)
                s = jnp.concatenate([s[:, : b - a - HALF], last], 1) if b - a > HALF else last
            kept.append(s)
            for k in range(0, b - a, HALF):
                part = s[:, k : k + HALF]
                top = part if top is None else jnp.maximum(top, part)
            yield
        m = jnp.max(top, 1, keepdims=True) * SCALE_LOG2
        yield
        norm, out = None, None
        for i, (a, b) in enumerate(chunks):
            p = jnp.exp2(kept[i] * SCALE_LOG2 - m)
            kept[i] = p
            for k in range(0, b - a, HALF):
                part = p[:, k : k + HALF]
                norm = part if norm is None else norm + part
            pb = p.astype(bf16)
            p_s[u, :, a:b] = pb
            t = dot(pb, va[g, a:b], NN)
            out = t if out is None else out + t
            yield
        valid = jnp.concatenate([(rid + half * HALF < n).astype(f32)] * heads, 0)
        inv = valid / jnp.sum(norm, 1, keepdims=True)
        ob = (out * inv).astype(bf16)
        for c, s in zip(head_cols, head_rows):
            o_ref[0, rows, c] = ob[s]
        gh = jnp.concatenate([do_ref[0, rows, c] for c in head_cols], 0)
        gh = (gh.astype(f32) * inv).astype(bf16)
        g_s[u] = gh
        delta = jnp.sum(gh.astype(f32) * ob.astype(f32), 1, keepdims=True)
        yield
        grad = None
        for i, (a, b) in enumerate(chunks):
            x = dot(g_s[u], va[g, a:b], NT)
            ds = (kept[i] * (x - delta)).astype(bf16)
            ds_s[u, :, a:b] = ds
            t = dot(ds, ka[g, a:b], NN)
            grad = t if grad is None else grad + t
            yield
        grad = (grad * SCALE).astype(bf16)
        for c, s in zip(head_cols, head_rows):
            dq_ref[0, rows, c] = grad[s]
        for a, b in chunks:
            dv = dot(p_s[u, :, a:b], g_s[u], TN)
            dk = dot(ds_s[u, :, a:b], q_s[u], TN)
            if half == 0:
                dv_s[g, a:b], dk_s[g, a:b] = dv, dk
            else:
                e, f = min(b, first), max(a, first)
                if e > a:
                    dv_s[g, a:e] += dv[: e - a]
                    dk_s[g, a:e] += dk[: e - a]
                if b > f:
                    dv_s[g, f:b], dk_s[g, f:b] = dv[f - a :], dk[f - a :]
            yield

    chains = [chain(g, half) for g in range(kv_heads) for half in range(2)]
    live = list(range(len(chains)))
    step = 0
    while live:
        for i in list(live):
            if step >= i * LEAD and next(chains[i], chains) is chains:
                live.remove(i)
        step += 1
    pieces = (cores, block_rows, D)
    for g in range(kv_heads):
        cols = slice(g * D, (g + 1) * D)
        dk, dv = dk_s[g] * SCALE, dv_s[g]
        for k in range(parts):
            rows = slice(k * part_rows, (k + 1) * part_rows)
            dp_refs[k][:, :block_rows, cols] = dk[rows].astype(bf16).reshape(pieces)
            dp_refs[k][:, block_rows:, cols] = dv[rows].astype(bf16).reshape(pieces)
        dkr_ref[0, :, cols] = dk[prompt_len:].astype(bf16)
        dvr_ref[0, :, cols] = dv[prompt_len:].astype(bf16)


def attend(slot, lengths, queries, out_grad, resp_keys, resp_values, prompt_parts, done):
    D = HEAD_SIZE
    _, token_rows, width = queries.shape
    kv_width = resp_keys.shape[2]
    kv_heads = kv_width // D
    parts = len(prompt_parts)
    cores, both_rows, _ = prompt_parts[0].shape
    keys = parts * cores * both_rows // 2 + token_rows
    stack = width // kv_width * HALF

    def block(w):
        return pl.BlockSpec((1, token_rows, w), lambda i: (slot, 0, 0))

    sds = jax.ShapeDtypeStruct
    like = (queries, queries, resp_keys, resp_keys)
    outs = pl.pallas_call(
        functools.partial(attn_kernel, slot, parts),
        grid=(1,),
        in_specs=[SCALARS, WHOLE, block(width), WHOLE, WHOLE] + [WHOLE] * parts + [ANY] * len(done),
        out_specs=[block(x.shape[2]) for x in like] + [WHOLE] * parts,
        out_shape=[sds(x.shape, bf16) for x in like] + [sds(prompt_parts[0].shape, bf16)] * parts,
        input_output_aliases={5 + parts + i: i for i in range(len(done))},
        scratch_shapes=[
            pltpu.VMEM((2 * kv_heads, stack, keys), bf16),
            pltpu.VMEM((2 * kv_heads, stack, keys), bf16),
            pltpu.VMEM((2 * kv_heads, stack, D), bf16),
            pltpu.VMEM((2 * kv_heads, stack, D), bf16),
            pltpu.VMEM((kv_heads, keys, D), bf16),
            pltpu.VMEM((kv_heads, keys, D), bf16),
            pltpu.VMEM((kv_heads, keys, D), f32),
            pltpu.VMEM((kv_heads, keys, D), f32),
        ],
        compiler_params=pltpu.CompilerParams(
            vmem_limit_bytes=ATTN_VMEM, dimension_semantics=("arbitrary",)
        ),
        cost_estimate=pl.CostEstimate(
            flops=12 * token_rows * keys * width, bytes_accessed=8 * token_rows * width, transcendentals=0
        ),
        name="attn",
    )(lengths, queries, out_grad, resp_keys, resp_values, *prompt_parts, *done)
    return outs[:4], outs[4:]


def local(
    planes,
    queries,
    resp_keys,
    response_values,
    prompt_key_rows,
    prompt_value_rows,
    out_grad,
    group_list,
    lengths,
):
    dp = lax.axis_size("dp")
    per_plane = dp // planes
    chips = per_plane // 2
    count = queries.shape[0]
    me = lax.axis_index("dp")
    plane, chip, core = me // per_plane, me % per_plane // 2, me % 2

    def shift(v, k):
        return lax.ppermute(v, "dp", [(i, (i + k * per_plane) % dp) for i in range(dp)])


    def turn(v, k):
        pairs = [
            (i, i // per_plane * per_plane + (i % per_plane + 2 * k) % per_plane) for i in range(dp)
        ]
        return lax.ppermute(v, "dp", pairs)

    def swap(v):
        return lax.ppermute(v, "dp", [(i, i ^ 1) for i in range(dp)])

    there = (chip + jnp.arange(chips, dtype=jnp.int32)) % chips
    cores = jnp.stack([core, 1 - core])
    device = (plane * chips + there[None, :]) * 2 + cores[:, None]
    ids = (device[:, :, None] * count + jnp.arange(count, dtype=jnp.int32)).reshape(-1)
    member = group_list[:, :, None] == ids[None, None, :]
    above = (jnp.arange(planes, dtype=jnp.int32) - plane) % planes

    def by_prompt(value):
        return jnp.sum(jnp.where(member, value[:, None, None], 0), axis=(0, 1))

    key_rows, kv_width = prompt_key_rows.shape
    rows = 2 * key_rows
    zero = jnp.zeros((), bf16)
    mine = lax.pad(prompt_key_rows, zero, ((0, key_rows, 0), (0, 0, 0))) + lax.pad(
        prompt_value_rows, zero, ((key_rows, 0, 0), (0, 0, 0))
    )
    from2, from6 = shift(mine, -2), shift(mine, 2)
    late, from6 = lax.optimization_barrier((mine, from6))
    from4 = shift(late, 4)
    from1 = shift(jnp.concatenate([mine, from2], 0), -1)
    from7 = shift(jnp.concatenate([mine, from6], 0), 1)
    order = [0, 2, 6, 1, 3, 7, 5, 4]
    place = sum(jnp.where(above == d, at, 0) for at, d in enumerate(order))
    pieces = jnp.concatenate([mine, from2, from6, from1, from7, from4], 0).reshape(planes, rows, kv_width)
    partner = swap(pieces)
    sends = chips * count
    picked = pl.pallas_call(
        pick_kernel,
        in_specs=[SCALARS, WHOLE, WHOLE],
        out_specs=[WHOLE] * sends,
        out_shape=[jax.ShapeDtypeStruct((2, rows, kv_width), bf16)] * sends,
        compiler_params=pltpu.CompilerParams(vmem_limit_bytes=4 * 2**20),
        name="pick",
    )(by_prompt(place), pieces, partner)
    prompts = [
        [picked[r]] + [turn(picked[k * count + r], k) for k in range(1, chips)]
        for r in range(count)
    ]

    grads_in = [pltpu.with_memory_space_constraint(out_grad, pltpu.HBM)] + [out_grad] * (count - 1)
    written, grads = [], []
    for r in range(count):
        written, own = attend(
            r, lengths, queries, grads_in[r], resp_keys, response_values, prompts[r], written
        )
        grads.append(own)
    back = [jnp.stack([g[k] for g in grads]) for k in range(chips)]
    back = jnp.stack([back[0]] + [turn(back[k], -k) for k in range(1, chips)])
    terms = [back[:, r, 0] for r in range(count)]
    partner = swap(back[:, :, 1])
    partner_terms = [partner[:, r] for r in range(count)]
    attn_out, grad_q, grad_k, grad_v = written

    by_slot = by_prompt(above).reshape(2, chips, count).transpose(0, 2, 1).reshape(-1)
    sds = jax.ShapeDtypeStruct
    up, down, far, keep = pl.pallas_call(
        fold_kernel,
        in_specs=[SCALARS] + [WHOLE] * (2 * count),
        out_specs=[WHOLE] * 4,
        out_shape=[
            sds((2, rows, kv_width), bf16),
            sds((2, rows, kv_width), bf16),
            sds((rows, kv_width), bf16),
            sds((3, rows, kv_width), f32),
        ],
        scratch_shapes=[pltpu.VMEM((planes, rows, kv_width), f32)],
        compiler_params=pltpu.CompilerParams(vmem_limit_bytes=8 * 2**20),
        name="fold",
    )(by_slot, *terms, *partner_terms)
    up, down = shift(up, 1), shift(down, -1)
    far = shift(far, 4)
    up2 = shift((keep[1] + up[1].astype(f32)).astype(bf16), 2)
    down2 = shift((keep[2] + down[1].astype(f32)).astype(bf16), -2)
    near = keep[0] + up[0].astype(f32) + down[0].astype(f32)
    total = near + up2.astype(f32) + down2.astype(f32) + far.astype(f32)
    total = total.astype(bf16)
    return attn_out, grad_q, grad_k, grad_v, total[:key_rows], total[key_rows:]


def solution(mesh):
    in_specs = (
        P("dp", None, "tensor"),
        P("dp", None, "tensor"),
        P("dp", None, "tensor"),
        P("dp", "tensor"),
        P("dp", "tensor"),
        P("dp", None, "tensor"),
        P(),
        P("dp"),
    )
    out_specs = (
        P("dp", None, "tensor"),
        P("dp", None, "tensor"),
        P("dp", None, "tensor"),
        P("dp", None, "tensor"),
        P("dp", "tensor"),
        P("dp", "tensor"),
    )

    def step(*args):
        planes = args[6].shape[0]
        return jax.shard_map(
            functools.partial(local, planes),
            mesh=mesh,
            in_specs=in_specs,
            out_specs=out_specs,
            check_vma=False,
        )(*args)

    return step
```

```python
import functools
import math

import jax
import jax.numpy as jnp
from jax import lax
from jax.experimental import pallas as pl
from jax.experimental.pallas import tpu as pltpu
from jax.sharding import PartitionSpec as P

HEAD_SIZE = 128
SCALE = HEAD_SIZE**-0.5
SCALE_LOG2 = SCALE * math.log2(math.e)
HALF = 128
CHUNK = 256
LEAD = 3
ATTN_VMEM = 28 * 2**20
NT = (((1,), (1,)), ((), ()))
NN = (((1,), (0,)), ((), ()))
TN = (((0,), (0,)), ((), ()))
f32 = jnp.float32
bf16 = jnp.bfloat16
WHOLE = pl.BlockSpec(memory_space=pltpu.VMEM)
ANY = pl.BlockSpec(memory_space=pl.ANY)
HBM = pl.BlockSpec(memory_space=pltpu.HBM)
SCALARS = pl.BlockSpec(memory_space=pltpu.SMEM)


def dot(a, b, dims):
    return lax.dot_general(a, b, dims, preferred_element_type=f32)


def pick_kernel(idx_ref, own_ref, partner_ref, *outs):
    for i, out in enumerate(outs):
        block = idx_ref[i]
        out[0] = own_ref[block]
        out[1] = partner_ref[block]


def fold_kernel(idx_ref, *refs):
    *terms, up_ref, down_ref, far_ref, keep_ref, total = refs
    total[...] = jnp.zeros_like(total)
    at = 0
    for term in terms:
        for k in range(term.shape[0]):
            d = idx_ref[at]
            total[d] = total[d] + term[k].astype(f32)
            at += 1
    up_ref[0], up_ref[1] = total[1].astype(bf16), total[3].astype(bf16)
    down_ref[0], down_ref[1] = total[7].astype(bf16), total[5].astype(bf16)
    far_ref[...] = total[4].astype(bf16)
    keep_ref[0], keep_ref[1], keep_ref[2] = total[0], total[2], total[6]


def attn_kernel(slot, parts, len_ref, q_ref, do_ref, kr_ref, vr_ref, *refs):
    part_refs, refs = refs[:parts], refs[parts:]
    refs = refs[0 if slot == 0 else 4 :]
    o_ref, dq_ref, dkr_ref, dvr_ref, *refs = refs
    dp_refs, refs = refs[:parts], refs[parts:]
    p_s, ds_s, g_s, q_s, ka, va, dk_s, dv_s = refs
    D = HEAD_SIZE
    kv_heads = kr_ref.shape[2] // D
    heads = q_ref.shape[2] // (D * kv_heads)
    cores, both_rows, _ = part_refs[0].shape
    block_rows = both_rows // 2
    part_rows = cores * block_rows
    prompt_len = parts * part_rows
    n = len_ref[slot]
    for g in range(kv_heads):
        cols = slice(g * D, (g + 1) * D)
        for k in range(parts):
            rows = slice(k * part_rows, (k + 1) * part_rows)
            ka[g, rows] = part_refs[k][:, :block_rows, cols].reshape(part_rows, D)
            va[g, rows] = part_refs[k][:, block_rows:, cols].reshape(part_rows, D)
        ka[g, prompt_len:] = kr_ref[slot, :, cols]
        va[g, prompt_len:] = vr_ref[slot, :, cols]
    row = lax.broadcasted_iota(jnp.int32, (HALF, HALF), 0)
    col = lax.broadcasted_iota(jnp.int32, (HALF, HALF), 1)
    tri = jnp.concatenate([col <= row] * heads, 0)
    rid = lax.broadcasted_iota(jnp.int32, (HALF, 1), 0)
    first = prompt_len + HALF

    def chain(g, half):
        u = 2 * g + half
        j = first + HALF * half
        rows = slice(half * HALF, (half + 1) * HALF)
        head_cols = [slice((g * heads + h) * D, (g * heads + h + 1) * D) for h in range(heads)]
        head_rows = [slice(h * HALF, (h + 1) * HALF) for h in range(heads)]
        q_s[u] = jnp.concatenate([q_ref[slot, rows, c] for c in head_cols], 0)
        chunks = [(a, min(a + CHUNK, j)) for a in range(0, j, CHUNK)]
        top, kept = None, []
        for a, b in chunks:
            s = dot(q_s[u], ka[g, a:b], NT)
            if b == j:
                last = jnp.where(tri, s[:, b - a - HALF :], -jnp.inf)
                s = jnp.concatenate([s[:, : b - a - HALF], last], 1) if b - a > HALF else last
            kept.append(s)
            for k in range(0, b - a, HALF):
                part = s[:, k : k + HALF]
                top = part if top is None else jnp.maximum(top, part)
            yield
        m = jnp.max(top, 1, keepdims=True) * SCALE_LOG2
        yield
        norm, out = None, None
        for i, (a, b) in enumerate(chunks):
            p = jnp.exp2(kept[i] * SCALE_LOG2 - m)
            kept[i] = p
            for k in range(0, b - a, HALF):
                part = p[:, k : k + HALF]
                norm = part if norm is None else norm + part
            pb = p.astype(bf16)
            p_s[u, :, a:b] = pb
            t = dot(pb, va[g, a:b], NN)
            out = t if out is None else out + t
            yield
        valid = jnp.concatenate([(rid + half * HALF < n).astype(f32)] * heads, 0)
        inv = valid / jnp.sum(norm, 1, keepdims=True)
        ob = (out * inv).astype(bf16)
        for c, s in zip(head_cols, head_rows):
            o_ref[0, rows, c] = ob[s]
        gh = jnp.concatenate([do_ref[0, rows, c] for c in head_cols], 0)
        gh = (gh.astype(f32) * inv).astype(bf16)
        g_s[u] = gh
        delta = jnp.sum(gh.astype(f32) * ob.astype(f32), 1, keepdims=True)
        yield
        grad = None
        for i, (a, b) in enumerate(chunks):
            x = dot(g_s[u], va[g, a:b], NT)
            ds = (kept[i] * (x - delta)).astype(bf16)
            ds_s[u, :, a:b] = ds
            t = dot(ds, ka[g, a:b], NN)
            grad = t if grad is None else grad + t
            yield
        grad = (grad * SCALE).astype(bf16)
        for c, s in zip(head_cols, head_rows):
            dq_ref[0, rows, c] = grad[s]
        for a, b in chunks:
            dv = dot(p_s[u, :, a:b], g_s[u], TN)
            dk = dot(ds_s[u, :, a:b], q_s[u], TN)
            if half == 0:
                dv_s[g, a:b], dk_s[g, a:b] = dv, dk
            else:
                e, f = min(b, first), max(a, first)
                if e > a:
                    dv_s[g, a:e] += dv[: e - a]
                    dk_s[g, a:e] += dk[: e - a]
                if b > f:
                    dv_s[g, f:b], dk_s[g, f:b] = dv[f - a :], dk[f - a :]
            yield

    chains = [chain(g, half) for g in range(kv_heads) for half in range(2)]
    live = list(range(len(chains)))
    step = 0
    while live:
        for i in list(live):
            if step >= i * LEAD and next(chains[i], chains) is chains:
                live.remove(i)
        step += 1
    pieces = (cores, block_rows, D)
    for g in range(kv_heads):
        cols = slice(g * D, (g + 1) * D)
        dk, dv = dk_s[g] * SCALE, dv_s[g]
        for k in range(parts):
            rows = slice(k * part_rows, (k + 1) * part_rows)
            dp_refs[k][:, :block_rows, cols] = dk[rows].astype(bf16).reshape(pieces)
            dp_refs[k][:, block_rows:, cols] = dv[rows].astype(bf16).reshape(pieces)
        dkr_ref[0, :, cols] = dk[prompt_len:].astype(bf16)
        dvr_ref[0, :, cols] = dv[prompt_len:].astype(bf16)


def attend(slot, lengths, queries, out_grad, resp_keys, resp_values, prompt_parts, done):
    D = HEAD_SIZE
    _, token_rows, width = queries.shape
    kv_width = resp_keys.shape[2]
    kv_heads = kv_width // D
    parts = len(prompt_parts)
    cores, both_rows, _ = prompt_parts[0].shape
    keys = parts * cores * both_rows // 2 + token_rows
    stack = width // kv_width * HALF

    def block(w):
        return pl.BlockSpec((1, token_rows, w), lambda i: (slot, 0, 0))

    sds = jax.ShapeDtypeStruct
    like = (queries, queries, resp_keys, resp_keys)
    outs = pl.pallas_call(
        functools.partial(attn_kernel, slot, parts),
        grid=(1,),
        in_specs=[SCALARS, WHOLE, block(width), WHOLE, WHOLE] + [WHOLE] * parts + [ANY] * len(done),
        out_specs=[block(x.shape[2]) for x in like] + [WHOLE] * parts,
        out_shape=[sds(x.shape, bf16) for x in like] + [sds(prompt_parts[0].shape, bf16)] * parts,
        input_output_aliases={5 + parts + i: i for i in range(len(done))},
        scratch_shapes=[
            pltpu.VMEM((2 * kv_heads, stack, keys), bf16),
            pltpu.VMEM((2 * kv_heads, stack, keys), bf16),
            pltpu.VMEM((2 * kv_heads, stack, D), bf16),
            pltpu.VMEM((2 * kv_heads, stack, D), bf16),
            pltpu.VMEM((kv_heads, keys, D), bf16),
            pltpu.VMEM((kv_heads, keys, D), bf16),
            pltpu.VMEM((kv_heads, keys, D), f32),
            pltpu.VMEM((kv_heads, keys, D), f32),
        ],
        compiler_params=pltpu.CompilerParams(
            vmem_limit_bytes=ATTN_VMEM, dimension_semantics=("arbitrary",)
        ),
        cost_estimate=pl.CostEstimate(
            flops=12 * token_rows * keys * width, bytes_accessed=8 * token_rows * width, transcendentals=0
        ),
        name="attn",
    )(lengths, queries, out_grad, resp_keys, resp_values, *prompt_parts, *done)
    return outs[:4], outs[4:]


def local(
    planes,
    queries,
    resp_keys,
    response_values,
    prompt_key_rows,
    prompt_value_rows,
    out_grad,
    group_list,
    lengths,
):
    dp = lax.axis_size("dp")
    per_plane = dp // planes
    chips = per_plane // 2
    count = queries.shape[0]
    me = lax.axis_index("dp")
    plane, chip, core = me // per_plane, me % per_plane // 2, me % 2

    def shift(v, k):
        return lax.ppermute(v, "dp", [(i, (i + k * per_plane) % dp) for i in range(dp)])


    def turn(v, k):
        pairs = [
            (i, i // per_plane * per_plane + (i % per_plane + 2 * k) % per_plane) for i in range(dp)
        ]
        return lax.ppermute(v, "dp", pairs)

    def swap(v):
        return lax.ppermute(v, "dp", [(i, i ^ 1) for i in range(dp)])

    there = (chip + jnp.arange(chips, dtype=jnp.int32)) % chips
    cores = jnp.stack([core, 1 - core])
    device = (plane * chips + there[None, :]) * 2 + cores[:, None]
    ids = (device[:, :, None] * count + jnp.arange(count, dtype=jnp.int32)).reshape(-1)
    member = group_list[:, :, None] == ids[None, None, :]
    above = (jnp.arange(planes, dtype=jnp.int32) - plane) % planes

    def by_prompt(value):
        return jnp.sum(jnp.where(member, value[:, None, None], 0), axis=(0, 1))

    key_rows, kv_width = prompt_key_rows.shape
    rows = 2 * key_rows
    zero = jnp.zeros((), bf16)
    mine = lax.pad(prompt_key_rows, zero, ((0, key_rows, 0), (0, 0, 0))) + lax.pad(
        prompt_value_rows, zero, ((key_rows, 0, 0), (0, 0, 0))
    )
    from2, from6 = shift(mine, -2), shift(mine, 2)
    late, from6 = lax.optimization_barrier((mine, from6))
    from4 = shift(late, 4)
    from1 = shift(jnp.concatenate([mine, from2], 0), -1)
    from7 = shift(jnp.concatenate([mine, from6], 0), 1)
    order = [0, 2, 6, 1, 3, 7, 5, 4]
    place = sum(jnp.where(above == d, at, 0) for at, d in enumerate(order))
    pieces = jnp.concatenate([mine, from2, from6, from1, from7, from4], 0).reshape(planes, rows, kv_width)
    first = swap(jnp.concatenate([mine, from2, from6], 0))
    rest = swap(jnp.concatenate([from1, from7, from4], 0))
    partner = jnp.concatenate([first, rest], 0).reshape(pieces.shape)
    sends = chips * count
    picked = pl.pallas_call(
        pick_kernel,
        in_specs=[SCALARS, WHOLE, WHOLE],
        out_specs=[WHOLE] * sends,
        out_shape=[jax.ShapeDtypeStruct((2, rows, kv_width), bf16)] * sends,
        compiler_params=pltpu.CompilerParams(vmem_limit_bytes=4 * 2**20),
        name="pick",
    )(by_prompt(place), pieces, partner)
    prompts = [
        [picked[r]] + [turn(picked[k * count + r], k) for k in range(1, chips)]
        for r in range(count)
    ]

    grads_in = [pltpu.with_memory_space_constraint(out_grad, pltpu.HBM)] + [out_grad] * (count - 1)
    written, grads = [], []
    for r in range(count):
        written, own = attend(
            r, lengths, queries, grads_in[r], resp_keys, response_values, prompts[r], written
        )
        grads.append(own)
    back = [jnp.stack([g[k] for g in grads]) for k in range(chips)]
    back = jnp.stack([back[0]] + [turn(back[k], -k) for k in range(1, chips)])
    terms = [back[:, r, 0] for r in range(count)]
    partner = swap(back[:, :, 1])
    partner_terms = [partner[:, r] for r in range(count)]
    attn_out, grad_q, grad_k, grad_v = written

    by_slot = by_prompt(above).reshape(2, chips, count).transpose(0, 2, 1).reshape(-1)
    sds = jax.ShapeDtypeStruct
    up, down, far, keep = pl.pallas_call(
        fold_kernel,
        in_specs=[SCALARS] + [WHOLE] * (2 * count),
        out_specs=[WHOLE] * 4,
        out_shape=[
            sds((2, rows, kv_width), bf16),
            sds((2, rows, kv_width), bf16),
            sds((rows, kv_width), bf16),
            sds((3, rows, kv_width), f32),
        ],
        scratch_shapes=[pltpu.VMEM((planes, rows, kv_width), f32)],
        compiler_params=pltpu.CompilerParams(vmem_limit_bytes=8 * 2**20),
        name="fold",
    )(by_slot, *terms, *partner_terms)
    up, down = shift(up, 1), shift(down, -1)
    far = shift(far, 4)
    up2 = shift((keep[1] + up[1].astype(f32)).astype(bf16), 2)
    down2 = shift((keep[2] + down[1].astype(f32)).astype(bf16), -2)
    near = keep[0] + up[0].astype(f32) + down[0].astype(f32)
    total = near + up2.astype(f32) + down2.astype(f32) + far.astype(f32)
    total = total.astype(bf16)
    return attn_out, grad_q, grad_k, grad_v, total[:key_rows], total[key_rows:]


def solution(mesh):
    in_specs = (
        P("dp", None, "tensor"),
        P("dp", None, "tensor"),
        P("dp", None, "tensor"),
        P("dp", "tensor"),
        P("dp", "tensor"),
        P("dp", None, "tensor"),
        P(),
        P("dp"),
    )
    out_specs = (
        P("dp", None, "tensor"),
        P("dp", None, "tensor"),
        P("dp", None, "tensor"),
        P("dp", None, "tensor"),
        P("dp", "tensor"),
        P("dp", "tensor"),
    )

    def step(*args):
        planes = args[6].shape[0]
        return jax.shard_map(
            functools.partial(local, planes),
            mesh=mesh,
            in_specs=in_specs,
            out_specs=out_specs,
            check_vma=False,
        )(*args)

    return step
```
